256 devices in a mesh: dp: 4 (over x), owner: 64 (over y, z, core).
Axes of the slice: x: 4, y: 4, z: 8, core: 2. Of those that a mesh axis runs over, the one named last changes fastest.
Arguments:
- vectors: bfloat16 [196608, 1024], P(('dp', 'owner')), may hold values from -6 to 6
- meso_labels: int32 [196608], P(('dp', 'owner')), may hold values from 0 to 2047, as said below
- fine_labels: int32 [196608], P(('dp', 'owner')), may hold values from 0 to 63
- meso_centroids: float32 [2048, 1024], P('owner'), may hold values from -6 to 6
- fine_centroids: bfloat16 [2048, 64, 1024], P('owner'), may hold values from -4 to 4
Outputs:
- nearest: float32 [196608], P(('dp', 'owner'))
- new_meso: float32 [2048, 1024], P('owner')
- new_fine: float32 [2048, 64, 1024], P('owner', 'dp')
The draws below stay inside these ranges and needn't reach their ends.
Inputs may be any that keep to these rules, and one draw needn't show every extreme that they name: `meso_labels`: each vector's mesocluster lies in the block of 32 owned by one index of owner; among the vectors of one device, those whose mesocluster belongs to one owner and whose fine label lies in one aligned block of 16 number at most 6, and this many in every draw.
All inputs are finite; a program needn't handle non-finite values.
Results may differ from the reference program's by a relative error of at most 0.0003.
Values may be sent and summed in bfloat16 or wider, within the bound.
A program may use at most 64 MiB of HBM per device.

```python
import jax
import jax.numpy as jnp
from jax import lax

D = 1024
KF = 64
MESO_DEV = 32
ROWS_DEV = 768
MESO = 2048
FGROUP = 16
SLOTS = 6
N_ROWS = 196608
N_DP = 4
N_OWNER = 64


def route_labels(key):
    bin_total = N_OWNER * N_DP
    slot_total = bin_total * SLOTS
    devices = N_ROWS // ROWS_DEV
    popular = jax.random.permutation(jax.random.fold_in(key, 11), N_OWNER) < N_OWNER // 4
    slot_ids = jnp.arange(slot_total, dtype=jnp.int32)
    slot_owner = slot_ids // (N_DP * SLOTS)
    noise_ints = jax.random.randint(jax.random.fold_in(key, 12), (devices, slot_total), 0, 2 ** 18, dtype=jnp.int32)
    slot_score = jnp.where(popular[slot_owner][None, :], 2 ** 30 + slot_ids[None, :], noise_ints * slot_total + slot_ids[None, :])
    chosen = lax.top_k(slot_score, ROWS_DEV)[1].astype(jnp.int32)
    row_keys = jax.random.split(jax.random.fold_in(key, 13), devices)
    row_order = jax.vmap(lambda sub_key: jax.random.permutation(sub_key, ROWS_DEV))(row_keys).astype(jnp.int32)
    chosen = jnp.take_along_axis(chosen, row_order, axis=1)
    owner_of = chosen // (N_DP * SLOTS)
    group_of = chosen // SLOTS % N_DP
    meso_ids = owner_of * MESO_DEV + jax.random.randint(jax.random.fold_in(key, 14), (devices, ROWS_DEV), 0, MESO_DEV, dtype=jnp.int32)
    fine_ids = group_of * FGROUP + jax.random.randint(jax.random.fold_in(key, 15), (devices, ROWS_DEV), 0, FGROUP, dtype=jnp.int32)
    return (meso_ids.reshape(-1), fine_ids.reshape(-1))


def draw_meso_labels(key, part):
    labels = route_labels(key)
    return labels[0]


def draw_fine_labels(key, part):
    labels = route_labels(key)
    return labels[1]


def shard_levels(rng, shape, cuts, smallest, top_value):
    loudness, own = 1.0, jax.random.fold_in(rng, 6)
    for axis_at, blocks in cuts:
        heights = jnp.exp(jax.random.uniform(jax.random.fold_in(own, axis_at), (blocks,), jnp.float32, smallest / len(cuts), top_value / len(cuts)))
        loudness = loudness * jnp.repeat(heights, shape[axis_at] // blocks).reshape([-1 if axis == axis_at else 1 for axis in range(len(shape))])
    return loudness


def gaussian(rng, extent, deviation, bound, shards=(), kind=jnp.bfloat16):
    entries = jax.random.normal(rng, extent, jnp.float32) * deviation
    if len(shards) > 0:
        entries = shard_levels(rng, extent, shards, -0.22, 0.18) * entries
    return jnp.clip(entries, min=-bound, max=bound).astype(kind)


def setup_inputs(seed: int = 0) -> dict:
    seeds = jax.random.split(jax.random.key(seed), 6)
    return {
        "vectors": gaussian(seeds[0], (N_ROWS, D), 1.0, 6.0, ((0, 256),)),
        "meso_labels": draw_meso_labels(jax.random.fold_in(seeds[5], 71), 0),
        "fine_labels": draw_fine_labels(jax.random.fold_in(seeds[5], 71), 0),
        "meso_centroids": gaussian(seeds[3], (MESO, D), 1.0, 6.0, ((0, 64),), jnp.float32),
        "fine_centroids": gaussian(seeds[4], (MESO, KF, D), 0.5, 4.0, ((0, 64),)),
    }


smoothing = 1.0


def reference(vectors, meso_labels, fine_labels, meso_centroids, fine_centroids):
    block_rows = 256
    vector_blocks = vectors.reshape(-1, block_rows, D)
    label_blocks = meso_labels.reshape(-1, block_rows)

    def score_block(inputs):
        row_block, labels = inputs
        centroids = fine_centroids[labels].astype(jnp.float32)
        wide_rows = row_block.astype(jnp.float32)
        cross_terms = jnp.einsum("rd,rkd->rk", wide_rows, centroids)
        cent_norms = jnp.einsum("rkd,rkd->rk", centroids, centroids)
        row_norms = jnp.einsum("rd,rd->r", wide_rows, wide_rows)
        distance = row_norms[:, None] - 2.0 * cross_terms + cent_norms
        return jnp.min(distance, axis=1) / D

    nearest = lax.map(score_block, (vector_blocks, label_blocks)).reshape(-1)
    code_words = (meso_labels * KF + fine_labels).astype(jnp.int32)
    fine_sum = jax.ops.segment_sum(vectors.astype(jnp.float32), code_words, num_segments=MESO * KF).reshape(MESO, KF, D)
    fine_count = jax.ops.segment_sum(jnp.ones(code_words.shape, jnp.float32), code_words, num_segments=MESO * KF).reshape(MESO, KF)
    meso_sum = jnp.sum(fine_sum, axis=1)
    meso_count = jnp.sum(fine_count, axis=1)
    new_meso = (meso_sum + smoothing * meso_centroids) / (meso_count[:, None] + smoothing)
    meso_shift = new_meso - meso_centroids
    new_fine = (fine_sum + smoothing * (fine_centroids.astype(jnp.float32) + meso_shift[:, None, :])) / (fine_count[:, :, None] + smoothing)
    return nearest, new_meso, new_fine
```

```python
import functools

import jax
import jax.numpy as jnp
from jax import lax
from jax.experimental import pallas as pl
from jax.experimental.pallas import tpu as pltpu
from jax.sharding import PartitionSpec as P

MESH = pl.DeviceIdType.MESH
D = 1024
ROWS = 768
KF = 64
MESO_DEV = 32
FGROUP = 16
SLOTS = 6
NX, NY, NZ, NC = 4, 4, 8, 2
CHUNKS = NY
WAYS = 8
BLOCK = WAYS * SLOTS
CHUNK_ROWS = WAYS * BLOCK
BINS = CHUNKS * WAYS * WAYS
LANES = 128
KIND = ("zx", "zx", "zx", "xz")
ORDER = (0, 3, 1, 2)

F32, BF16, I32 = jnp.float32, jnp.bfloat16, jnp.int32
NT = (((1,), (1,)), ((), ()))
TN = (((0,), (0,)), ((), ()))


def iota(shape, dim):
    return lax.broadcasted_iota(I32, shape, dim)


def div6(v):
    return (v * 10923) >> 16


def div48(v):
    return div6(v >> 3)


def split3(v):
    first = v.astype(BF16)
    rest = v - first.astype(F32)
    second = rest.astype(BF16)
    third = (rest - second.astype(F32)).astype(BF16)
    return (first, second, third)


def dot(a, b, dims=(((1,), (0,)), ((), ()))):
    return lax.dot_general(a, b, dims, preferred_element_type=F32)


def kernel(
    meso_ref, fine_ref, vec_hbm, old_hbm, cent_hbm,
    near_ref, new_meso_ref, new_fine_ref,
    vec, old, cent, half_norm, perm, packed, got1, mid, got2,
    code1, code1_got, code2, ret1, ret1_got, ret2,
    sums, counts, msum, mcount, part, part_got,
    load_sem, s1_send, s1_recv, s2_send, s2_recv, c1_send, c1_recv, c2_send, c2_recv,
    r1_send, r1_recv, r2_send, r2_recv, p_send, p_recv,
):
    x = lax.axis_index("dp")
    own = lax.axis_index("owner")
    y, z, c = own // 16, lax.rem(own // 2, 8), lax.rem(own, 2)

    def yz_peer(dy, dz):
        return (x, (lax.rem(y + dy, NY) * NZ + lax.rem(z + dz, NZ)) * NC + c)

    def xc_peer(j):
        return (lax.rem(x + j // NC, NX), (y * NZ + z) * NC + lax.rem(c + j % NC, NC))

    def peer(q, hop, way):
        over_z = (KIND[q] == "zx") == (hop == 1)
        if over_z:
            return None if q == 0 and way == 0 else yz_peer(q, way)
        return None if way == 0 else xc_peer(way)

    def peer_back(q, hop, way):
        over_z = (KIND[q] == "zx") == (hop == 1)
        if over_z:
            return None if q == 0 and way == 0 else yz_peer((NY - q) % NY, (NZ - way) % NZ)
        return None if way == 0 else xc_peer(((NX - way // NC) % NX) * NC + way % NC)

    sent = []

    def send(src, dst, send_sem, recv_sem, device):
        copy = pltpu.make_async_remote_copy(
            src_ref=src, dst_ref=dst, send_sem=send_sem, recv_sem=recv_sem,
            device_id=device, device_id_type=MESH,
        )
        copy.start()
        sent.append(copy)

    def arrived(dst, send_sem, recv_sem):
        pltpu.make_async_remote_copy(
            src_ref=dst, dst_ref=dst, send_sem=send_sem, recv_sem=recv_sem,
            device_id=(x, own), device_id_type=MESH,
        ).wait_recv()

    load_vec = pltpu.make_async_copy(vec_hbm, vec, load_sem.at[0])
    load_cent = pltpu.make_async_copy(cent_hbm, cent, load_sem.at[1])
    load_old = pltpu.make_async_copy(old_hbm, old, load_sem.at[2])
    load_vec.start()
    load_cent.start()
    load_old.start()

    barrier = pltpu.get_barrier_semaphore()
    partners = 0
    for dy in range(NY):
        for dz in range(NZ):
            if dy or dz:
                pl.semaphore_signal(barrier, 1, device_id=yz_peer(dy, dz), device_id_type=MESH)
                partners += 1
    for j in range(1, WAYS):
        pl.semaphore_signal(barrier, 1, device_id=xc_peer(j), device_id_type=MESH)
        partners += 1

    meso = meso_ref[...]
    fine = fine_ref[...]
    to = meso >> 5
    dy = ((to >> 4) - y) & 3
    dz = (((to >> 1) & 7) - z) & 7
    way = ((((fine >> 4) - x) & 3) << 1) + ((to - c) & 1)
    x_first = functools.reduce(jnp.logical_or, [dy == q for q in range(CHUNKS) if KIND[q] == "xz"])
    hop1 = jnp.where(x_first, way, dz)
    hop2 = jnp.where(x_first, dz, way)
    first = (dy << 3) + hop1
    bin_of = (first << 3) + hop2
    in_bin = iota((BINS, ROWS), 0) == bin_of
    bin_hot = in_bin.astype(F32).astype(BF16)
    before = (iota((ROWS, ROWS), 0) < iota((ROWS, ROWS), 1)).astype(F32).astype(BF16)
    rank = jnp.sum(jnp.where(in_bin, dot(bin_hot, before), 0.0), axis=0, keepdims=True).astype(I32)
    slot = bin_of * SLOTS + rank

    first_hit = iota((CHUNKS * WAYS, ROWS), 0) == first
    lane_hot = (iota((LANES, ROWS), 0) == hop2 * SLOTS + rank).astype(F32).astype(BF16)
    meso_rows = jnp.where(first_hit, ((meso & 31) + 1).astype(F32), 0.0).astype(BF16)
    fine_rows = jnp.where(first_hit, (fine & 15).astype(F32), 0.0).astype(BF16)
    codes = 16.0 * dot(meso_rows, lane_hot, NT) + dot(fine_rows, lane_hot, NT) - 16.0
    for r in range(CHUNKS * WAYS):
        code1[r] = codes[r : r + 1, :]

    out_row = iota((CHUNK_ROWS, CHUNK_ROWS), 0)
    in_row = iota((CHUNK_ROWS, CHUNK_ROWS), 1)
    out_pair, in_pair = div6(out_row), div6(in_row)
    swapped = ((out_pair & 7) << 3) + (out_pair >> 3)
    perm[...] = (in_row - 6 * in_pair + 6 * swapped == out_row - 6 * out_pair + 6 * in_pair).astype(F32).astype(BF16)

    def pack(q):
        hot = (iota((CHUNK_ROWS, ROWS), 0) + q * CHUNK_ROWS == slot).astype(F32).astype(BF16)
        packed[q] = dot(hot, vec[...]).astype(BF16)

    def hop1_rows(q):
        for way in range(WAYS):
            at = q * WAYS + way
            rows = pl.ds(way * BLOCK, BLOCK)
            to = peer(q, 1, way)
            if to is None:
                got1[q, rows, :] = packed[q, rows, :]
            else:
                send(packed.at[q, rows], got1.at[q, rows], s1_send.at[at], s1_recv.at[at], to)

    load_vec.wait()
    pack(ORDER[0])
    pl.semaphore_wait(barrier, partners)
    for n, q in enumerate(ORDER):
        if n:
            pack(q)
        for way in range(WAYS):
            at = q * WAYS + way
            to = peer(q, 1, way)
            if to is None:
                code1_got[at] = code1[at]
            else:
                send(code1.at[at], code1_got.at[at], c1_send.at[at], c1_recv.at[at], to)
        hop1_rows(q)

    load_cent.wait()

    def norms(i, carry):
        rows = pl.ds(pl.multiple_of(i * 128, 128), 128)
        wide = cent[rows, :].astype(F32)
        half_norm[rows, :] = 0.5 * jnp.sum(wide * wide, axis=1, keepdims=True)
        return carry

    lax.fori_loop(0, MESO_DEV * KF // 128, norms, 0)
    sums[...] = jnp.zeros_like(sums)
    counts[...] = jnp.zeros_like(counts)
    msum[...] = jnp.zeros_like(msum)
    mcount[...] = jnp.zeros_like(mcount)

    def hop2_codes(q):
        for way in range(WAYS):
            at = q * WAYS + way
            if peer(q, 1, way) is not None:
                arrived(code1_got.at[at], c1_send.at[at], c1_recv.at[at])
        tile = pl.ds(q * WAYS, WAYS)
        for way in range(WAYS):
            at = q * WAYS + way
            to = peer(q, 2, way)
            if to is None:
                code2[pl.ds(at * WAYS, WAYS)] = code1_got[tile]
            else:
                send(code1_got.at[tile], code2.at[pl.ds(at * WAYS, WAYS)], c2_send.at[at], c2_recv.at[at], to)

    def hop2_rows(q):
        for way in range(WAYS):
            at = q * WAYS + way
            if peer(q, 1, way) is not None:
                arrived(got1.at[q, pl.ds(way * BLOCK, BLOCK)], s1_send.at[at], s1_recv.at[at])
        mid[q] = dot(perm[...], got1[q]).astype(BF16)
        for way in range(WAYS):
            at = q * WAYS + way
            rows = pl.ds(way * BLOCK, BLOCK)
            to = peer(q, 2, way)
            if to is None:
                got2[q, rows, :] = mid[q, rows, :]
            else:
                send(mid.at[q, rows], got2.at[q, rows], s2_send.at[at], s2_recv.at[at], to)

    lane_of = iota((LANES, CHUNK_ROWS), 1)
    code_lane = div48(lane_of) * SLOTS + lane_of - 6 * div6(lane_of)
    code_pick = (iota((LANES, CHUNK_ROWS), 0) == code_lane).astype(F32).astype(BF16)
    pair_hit = iota((WAYS * WAYS, CHUNK_ROWS), 0) == div6(iota((WAYS * WAYS, CHUNK_ROWS), 1))
    back_row = iota((CHUNK_ROWS, LANES), 0)
    back_pick = (iota((CHUNK_ROWS, LANES), 1) == back_row - 48 * div48(back_row)).astype(F32).astype(BF16)
    back_hit = iota((WAYS, CHUNK_ROWS), 0) == div48(iota((WAYS, CHUNK_ROWS), 1))
    eye = iota((128, 128), 0) == iota((128, 128), 1)

    def codes_of(q):
        tile = code2[pl.ds(q * WAYS * WAYS, WAYS * WAYS)].reshape(WAYS * WAYS, LANES).astype(I32)
        high = dot((tile >> 4).astype(F32).astype(BF16), code_pick)
        low = dot((tile & 15).astype(F32).astype(BF16), code_pick)
        high = jnp.sum(jnp.where(pair_hit, high, 0.0), axis=0, keepdims=True)
        low = jnp.sum(jnp.where(pair_hit, low, 0.0), axis=0, keepdims=True)
        return (high.astype(I32), low.astype(I32))

    def wait_chunk(q):
        for way in range(WAYS):
            at = q * WAYS + way
            if peer(q, 2, way) is not None:
                arrived(code2.at[pl.ds(at * WAYS, WAYS)], c2_send.at[at], c2_recv.at[at])
                arrived(got2.at[q, pl.ds(way * BLOCK, BLOCK)], s2_send.at[at], s2_recv.at[at])

    def add_meso(q, high):
        hot = (iota((MESO_DEV, CHUNK_ROWS), 0) == high).astype(F32)
        msum[...] += dot(hot.astype(BF16), got2[q])
        mcount[...] += jnp.sum(hot, axis=1, keepdims=True)

    def score(q, high):
        norm = jnp.concatenate(
            [
                jnp.sum(
                    jnp.where(eye, dot(got2[q, t : t + 128, :], got2[q, t : t + 128, :], NT), 0.0),
                    axis=0, keepdims=True,
                )
                for t in range(0, CHUNK_ROWS, 128)
            ],
            axis=1,
        )

        def block(i, best):
            rows = pl.ds(pl.multiple_of(i * 256, 256), 256)
            cross = dot(cent[rows, :], got2[q], NT) - half_norm[rows, :]
            for t in range(256 // KF):
                top = jnp.max(cross[t * KF : (t + 1) * KF], axis=0, keepdims=True)
                best = jnp.where(high == i * (256 // KF) + t, top, best)
            return best

        best = lax.fori_loop(0, MESO_DEV * KF // 256, block, jnp.zeros((1, CHUNK_ROWS), F32))
        near = jnp.where(high >= 0, (norm - 2.0 * best) * (1.0 / D), 0.0)
        spread = sum(dot(part, back_pick) for part in split3(jnp.where(back_hit, near, 0.0)))
        for way in range(WAYS):
            at = q * WAYS + way
            ret1[at] = spread[way : way + 1, :]
            to = peer_back(q, 2, way)
            if to is None:
                ret1_got[at] = ret1[at]
            else:
                send(ret1.at[at], ret1_got.at[at], r1_send.at[at], r1_recv.at[at], to)

    def add_fine(q, high, low):
        code = (high << 4) + low

        def block(i, carry):
            rows = pl.ds(pl.multiple_of(i * 128, 128), 128)
            hot = (iota((128, CHUNK_ROWS), 0) + i * 128 == code).astype(F32)
            sums[rows, :] += dot(hot.astype(BF16), got2[q])
            counts[rows, :] += jnp.sum(hot, axis=1, keepdims=True)
            return carry

        lax.fori_loop(0, MESO_DEV * FGROUP // 128, block, 0)

    def pass_back(q):
        for way in range(WAYS):
            at = q * WAYS + way
            if peer(q, 2, way) is not None:
                arrived(ret1_got.at[at], r1_send.at[at], r1_recv.at[at])
        tile = pl.ds(q * WAYS, WAYS)
        for way in range(WAYS):
            at = q * WAYS + way
            to = peer_back(q, 1, way)
            if to is None:
                ret2[pl.ds(at * WAYS, WAYS)] = ret1_got[tile]
            else:
                send(ret1_got.at[tile], ret2.at[pl.ds(at * WAYS, WAYS)], r2_send.at[at], r2_recv.at[at], to)

    def work(q):
        wait_chunk(q)
        high, low = codes_of(q)
        add_meso(q, high)
        score(q, high)
        add_fine(q, high, low)

    for q in ORDER:
        hop2_codes(q)
    hop2_rows(3)
    hop2_rows(0)
    hop2_rows(1)
    work(0)
    hop2_rows(2)
    pass_back(0)
    work(1)
    pass_back(1)
    work(2)
    pass_back(2)

    wait_chunk(3)
    high, low = codes_of(3)
    add_meso(3, high)
    part[:, 0:D] = msum[...]
    part[:, D : D + LANES] = jnp.broadcast_to(mcount[...], (MESO_DEV, LANES))
    for dx in range(1, NX):
        send(part, part_got.at[dx - 1], p_send.at[dx - 1], p_recv.at[dx - 1], xc_peer(dx * NC))
    score(3, high)
    add_fine(3, high, low)
    pass_back(3)

    load_old.wait()
    for dx in range(1, NX):
        arrived(part_got.at[dx - 1], p_send.at[dx - 1], p_recv.at[dx - 1])
    total = (part[...] + part_got[1]) + (part_got[0] + part_got[2])
    new_meso_ref[...] = (total[:, 0:D] + old[...]) / (total[:, D : D + 1] + 1.0)

    def finish(m, carry):
        here = pl.ds(pl.multiple_of(m * FGROUP, FGROUP), FGROUP)
        mine = pl.ds(pl.multiple_of(m * KF + x * FGROUP, FGROUP), FGROUP)
        shift = new_meso_ref[pl.ds(m, 1), :] - old[pl.ds(m, 1), :]
        top = sums[here, :] + (cent[mine, :].astype(F32) + shift)
        new_fine_ref[here, :] = top / (counts[here, :] + 1.0)
        return carry

    lax.fori_loop(0, MESO_DEV, finish, 0)

    for q in range(CHUNKS):
        for way in range(WAYS):
            at = q * WAYS + way
            if peer(q, 1, way) is not None:
                arrived(ret2.at[pl.ds(at * WAYS, WAYS)], r2_send.at[at], r2_recv.at[at])
    back = ret2[...].reshape(BINS, LANES)
    picked = sum(dot(part, bin_hot, TN) for part in split3(back))
    mine = iota((LANES, ROWS), 0) == hop1 * SLOTS + rank
    near_ref[...] = jnp.sum(jnp.where(mine, picked, 0.0), axis=0, keepdims=True)

    for copy in sent:
        copy.wait_send()


def body(vectors, meso_labels, fine_labels, meso_centroids, fine_centroids):
    vmem = pl.BlockSpec(memory_space=pltpu.VMEM)
    hbm = pl.BlockSpec(memory_space=pl.ANY)
    hops = CHUNKS * WAYS
    dma = pltpu.SemaphoreType.DMA
    near, new_meso, new_fine = pl.pallas_call(
        kernel,
        out_shape=(
            jax.ShapeDtypeStruct((1, ROWS), F32),
            jax.ShapeDtypeStruct((MESO_DEV, D), F32),
            jax.ShapeDtypeStruct((MESO_DEV * FGROUP, D), F32),
        ),
        in_specs=[vmem, vmem, hbm, hbm, hbm],
        out_specs=(vmem, vmem, vmem),
        scratch_shapes=[
            pltpu.VMEM((ROWS, D), BF16),
            pltpu.VMEM((MESO_DEV, D), F32),
            pltpu.VMEM((MESO_DEV * KF, D), BF16),
            pltpu.VMEM((MESO_DEV * KF, 1), F32),
            pltpu.VMEM((CHUNK_ROWS, CHUNK_ROWS), BF16),
            pltpu.VMEM((CHUNKS, CHUNK_ROWS, D), BF16),
            pltpu.VMEM((CHUNKS, CHUNK_ROWS, D), BF16),
            pltpu.VMEM((CHUNKS, CHUNK_ROWS, D), BF16),
            pltpu.VMEM((CHUNKS, CHUNK_ROWS, D), BF16),
            pltpu.VMEM((hops, 1, LANES), F32),
            pltpu.VMEM((hops, 1, LANES), F32),
            pltpu.VMEM((BINS, 1, LANES), F32),
            pltpu.VMEM((hops, 1, LANES), F32),
            pltpu.VMEM((hops, 1, LANES), F32),
            pltpu.VMEM((BINS, 1, LANES), F32),
            pltpu.VMEM((MESO_DEV * FGROUP, D), F32),
            pltpu.VMEM((MESO_DEV * FGROUP, 1), F32),
            pltpu.VMEM((MESO_DEV, D), F32),
            pltpu.VMEM((MESO_DEV, 1), F32),
            pltpu.VMEM((MESO_DEV, D + LANES), F32),
            pltpu.VMEM((NX - 1, MESO_DEV, D + LANES), F32),
            dma((3,)),
        ]
        + [dma((hops,)) for _ in range(12)]
        + [dma((NX - 1,)), dma((NX - 1,))],
        compiler_params=pltpu.CompilerParams(
            collective_id=0, has_side_effects=True, vmem_limit_bytes=56 * 2**20
        ),
    )(
        meso_labels.reshape(1, ROWS),
        fine_labels.reshape(1, ROWS),
        vectors,
        meso_centroids,
        fine_centroids.reshape(MESO_DEV * KF, D),
    )
    return (near.reshape(ROWS), new_meso, new_fine.reshape(MESO_DEV, FGROUP, D))


def solution(mesh):
    return jax.shard_map(
        body,
        mesh=mesh,
        in_specs=(
            P(("dp", "owner"), None),
            P(("dp", "owner")),
            P(("dp", "owner")),
            P("owner", None),
            P("owner", None, None),
        ),
        out_specs=(P(("dp", "owner")), P("owner", None), P("owner", "dp", None)),
        check_vma=False,
    )
```

```python
import jax
import jax.numpy as jnp
from jax import lax
from jax.experimental import pallas as pl
from jax.experimental.pallas import tpu as pltpu
from jax.sharding import PartitionSpec as P

MESH = pl.DeviceIdType.MESH
D = 1024
ROWS = 768
KF = 64
MESO_DEV = 32
FGROUP = 16
SLOTS = 6
NX, NY, NZ, NC = 4, 4, 8, 2
CHUNKS = NY
WAYS = 8
BLOCK = WAYS * SLOTS
CHUNK_ROWS = WAYS * BLOCK
BINS = CHUNKS * WAYS * WAYS
LANES = 128
SHARE = MESO_DEV // NX
SPLIT = 2
LATE = CHUNKS - SPLIT
EARLY = SPLIT * WAYS
LATER = LATE * WAYS
PAIRS = WAYS * WAYS
HALF = CHUNK_ROWS // 2

F32, BF16, I32 = jnp.float32, jnp.bfloat16, jnp.int32
NT = (((1,), (1,)), ((), ()))
TN = (((0,), (0,)), ((), ()))


def iota(shape, dim):
    return lax.broadcasted_iota(I32, shape, dim)


def div6(v):
    return (v * 10923) >> 16


def div48(v):
    return div6(v >> 3)


def split3(v):
    first = v.astype(BF16)
    rest = v - first.astype(F32)
    second = rest.astype(BF16)
    third = (rest - second.astype(F32)).astype(BF16)
    return (first, second, third)


def dot(a, b, dims=(((1,), (0,)), ((), ()))):
    return lax.dot_general(a, b, dims, preferred_element_type=F32)


def each(low, high, step):
    def body(i, carry):
        step(i)
        return carry

    lax.fori_loop(low, high, body, 0)


def kernel(
    meso_hbm, fine_hbm, vec_hbm, old_hbm, cent_hbm,
    near_ref, new_meso_ref, new_fine_ref,
    meso_ref, fine_ref, vec, old, cent, half_norm, perm, packed, got1, mid, got2,
    code1, code1_got, code2, last1, last1_got, last_mid, last2,
    ret1, ret1_got, ret_mid, back1, back1_got, ret2,
    sums, counts, msum, mcount, part, part_got, new_part, new_all,
    hot_ref, bin_hot, bin_ref, rank_ref, slot_ref,
    load_sem, s1_send, s1_recv, s2_send, s2_recv, c1_send, c1_recv, c2_send, c2_recv,
    r1_send, r1_recv, r2_send, r2_recv, p_send, p_recv, n_send, n_recv, gate,
):
    x = lax.axis_index("dp")
    own = lax.axis_index("owner")
    y, z, c = lax.div(own, 16), lax.rem(lax.div(own, 2), 8), lax.rem(own, 2)

    def yz_peer(dy, dz):
        return (x, (lax.rem(y + dy, NY) * NZ + lax.rem(z + dz, NZ)) * NC + c)

    def xc_peer(j):
        return (lax.rem(x + lax.div(j, NC), NX), (y * NZ + z) * NC + lax.rem(c + lax.rem(j, NC), NC))

    def xc_back(j):
        return (lax.rem(x + NX - lax.div(j, NC), NX), (y * NZ + z) * NC + lax.rem(c + lax.rem(j, NC), NC))

    def yz_back(dy, dz):
        return yz_peer(NY - dy, NZ - dz)

    def near_z(way):
        odd = lax.rem(way, 2)
        return lax.rem(odd * lax.div(way + 1, 2) + (1 - odd) * lax.div(2 * NZ - way, 2), NZ)

    def start_of(q):
        return lax.div(SPLIT - q, SPLIT)

    def link(src, dst, send_sem, recv_sem, device):
        return pltpu.make_async_remote_copy(
            src_ref=src, dst_ref=dst, send_sem=send_sem, recv_sem=recv_sem,
            device_id=device, device_id_type=MESH,
        )

    here = (x, own)

    def arrived(dst, send_sem, recv_sem):
        link(dst, dst, send_sem, recv_sem, here).wait_recv()

    def left(src, send_sem, recv_sem):
        link(src, src, send_sem, recv_sem, here).wait_send()

    def block(way):
        return pl.ds(pl.multiple_of(way * BLOCK, BLOCK), BLOCK)

    def ways(at):
        return pl.ds(at * WAYS, WAYS)

    barrier = pltpu.get_barrier_semaphore()

    def greet(device):
        pl.semaphore_signal(barrier, 1, device_id=device, device_id_type=MESH)

    each(1, NZ, lambda dz: greet(yz_peer(0, dz)))
    each(1, NY, lambda dy: greet(yz_peer(dy, 0)))
    each(1, WAYS, lambda j: greet(xc_peer(j)))
    greeted = NZ + NY + WAYS - 3

    load_meso = pltpu.make_async_copy(meso_hbm, meso_ref, load_sem.at[3])
    load_fine = pltpu.make_async_copy(fine_hbm, fine_ref, load_sem.at[4])
    load_vec = pltpu.make_async_copy(vec_hbm, vec, load_sem.at[0])
    load_cent = pltpu.make_async_copy(cent_hbm, cent, load_sem.at[1])
    load_old = pltpu.make_async_copy(old_hbm, old, load_sem.at[2])
    for load in (load_meso, load_fine, load_vec, load_cent, load_old):
        load.start()

    load_meso.wait()
    load_fine.wait()
    meso = meso_ref[...].reshape(1, ROWS)
    fine = fine_ref[...].reshape(1, ROWS)
    to = meso >> 5
    dy = ((to >> 4) - y) & 3
    dz = (((to >> 1) & 7) - z) & 7
    way = ((((fine >> 4) - x) & 3) << 1) + ((to - c) & 1)
    z_near = jnp.where(dz <= 4, jnp.maximum(2 * dz - 1, 0), 2 * (NZ - dz))
    is_last = dy >= SPLIT
    hop1 = jnp.where(is_last, way, dz)
    hop2 = jnp.where(is_last, z_near, way)
    first = (dy << 3) + hop1
    bin_of = (first << 3) + hop2
    bin_ref[...] = bin_of

    def bin_rows(i):
        rows = pl.ds(pl.multiple_of(i * 64, 64), 64)
        bin_hot[rows, :] = (iota((64, ROWS), 0) + i * 64 == bin_of).astype(F32).astype(BF16)

    each(0, BINS // 64, bin_rows)

    def ranks(i):
        lanes = pl.ds(pl.multiple_of(i * LANES, LANES), LANES)
        before = (iota((ROWS, LANES), 0) < iota((ROWS, LANES), 1) + i * LANES).astype(F32).astype(BF16)
        ahead = dot(bin_hot[...], before)
        mine = iota((BINS, LANES), 0) == bin_ref[:, lanes]
        rank_ref[:, lanes] = jnp.sum(jnp.where(mine, ahead, 0.0), axis=0, keepdims=True).astype(I32)

    each(0, ROWS // LANES, ranks)
    rank = rank_ref[...]
    slot_ref[...] = bin_of * SLOTS + rank

    meso_code = ((meso & 31) + 1).astype(F32)
    fine_code = (fine & 15).astype(F32)

    def code_rows(hit, lane):
        hot = (iota((LANES, ROWS), 0) == lane).astype(F32).astype(BF16)
        high = jnp.where(hit, meso_code, 0.0).astype(BF16)
        low = jnp.where(hit, fine_code, 0.0).astype(BF16)
        return 16.0 * dot(high, hot, NT) + dot(low, hot, NT)

    codes = code_rows(iota((EARLY, ROWS), 0) == first, hop2 * SLOTS + rank)
    for r in range(EARLY):
        code1[r] = codes[r : r + 1, :]
    codes = code_rows(iota((LATE * PAIRS, ROWS), 0) + SPLIT * PAIRS == bin_of, hop1 * SLOTS + rank)
    for r in range(LATE * PAIRS):
        last1[r] = codes[r : r + 1, :]

    load_vec.wait()

    def pack(q):
        def hot_rows(i):
            rows = pl.ds(pl.multiple_of(i * 64, 64), 64)
            at = iota((64, ROWS), 0) + (q * CHUNK_ROWS + i * 64)
            hot_ref[rows, :] = (at == slot_ref[...]).astype(F32).astype(BF16)

        def columns(i):
            lanes = pl.ds(pl.multiple_of(i * 256, 256), 256)
            packed[q, :, lanes] = dot(hot_ref[...], vec[:, lanes]).astype(BF16)

        each(0, CHUNK_ROWS // 64, hot_rows)
        each(0, D // 256, columns)

    def leave_late(q):
        late = q - SPLIT

        def code(way):
            at = late * WAYS + way
            link(last1.at[ways(at)], last1_got.at[ways(at)], c1_send.at[EARLY + at], c1_recv.at[EARLY + at], xc_peer(way)).start()

        def rows(way):
            at = q * WAYS + way
            link(packed.at[q, block(way)], got1.at[q, block(way)], s1_send.at[at], s1_recv.at[at], xc_peer(way)).start()

        last1_got[ways(late * WAYS)] = last1[ways(late * WAYS)]
        got1[q, 0:BLOCK, :] = packed[q, 0:BLOCK, :]
        each(1, WAYS, code)
        each(1, WAYS, rows)

    def leave_early(q):
        def code(way):
            at = q * WAYS + way
            link(code1.at[at], code1_got.at[at], c1_send.at[at], c1_recv.at[at], yz_peer(q, way)).start()

        def rows(way):
            at = q * WAYS + way
            link(packed.at[q, block(way)], got1.at[q, block(way)], s1_send.at[at], s1_recv.at[at], yz_peer(q, way)).start()

        each(start_of(q), WAYS, code)
        each(start_of(q), WAYS, rows)

    def pack_next(n):
        pack(lax.rem(n + SPLIT, CHUNKS))

    def signal(dy):
        pl.semaphore_signal(gate, 1, device_id=yz_peer(dy, 0), device_id_type=MESH)

    each(0, LATE + 1, pack_next)
    pl.semaphore_wait(barrier, greeted)
    code1_got[0] = code1[0]
    got1[0, 0:BLOCK, :] = packed[0, 0:BLOCK, :]
    leave_late(SPLIT)
    leave_early(0)
    each(1, NY, signal)
    each(SPLIT + 1, CHUNKS, leave_late)
    each(LATE + 1, CHUNKS, pack_next)
    pl.semaphore_wait(gate, NY - 1)
    each(1, SPLIT, leave_early)

    def perm_rows(i):
        rows = pl.ds(pl.multiple_of(i * 64, 64), 64)
        out_row = iota((64, CHUNK_ROWS), 0) + i * 64
        in_row = iota((64, CHUNK_ROWS), 1)
        out_pair, in_pair = div6(out_row), div6(in_row)
        swapped = ((out_pair & 7) << 3) + (out_pair >> 3)
        hit = in_row - 6 * in_pair + 6 * swapped == out_row - 6 * out_pair + 6 * in_pair
        perm[rows, :] = hit.astype(F32).astype(BF16)

    each(0, CHUNK_ROWS // 64, perm_rows)

    def regroup(q):
        def columns(i):
            lanes = pl.ds(pl.multiple_of(i * 256, 256), 256)
            mid[q, :, lanes] = dot(perm[...], got1[q, :, lanes]).astype(BF16)

        each(0, D // 256, columns)

    def pass_late(q):
        late = q - SPLIT

        def codes(way):
            at = late * WAYS + way
            arrived(last1_got.at[ways(at)], c1_send.at[EARLY + at], c1_recv.at[EARLY + at])

        def rows(way):
            at = q * WAYS + way
            arrived(got1.at[q, block(way)], s1_send.at[at], s1_recv.at[at])

        def codes_on(way):
            at = late * WAYS + way
            device = yz_peer(q, near_z(way))
            link(last_mid.at[at], last2.at[at], c2_send.at[EARLY + at], c2_recv.at[EARLY + at], device).start()

        def rows_on(way):
            at = q * WAYS + way
            device = yz_peer(q, near_z(way))
            link(mid.at[q, block(way)], got2.at[q, block(way)], s2_send.at[at], s2_recv.at[at], device).start()

        each(1, WAYS, codes)
        last_mid[ways(late)] = sum(last1_got[pl.ds(late * PAIRS + way * WAYS, WAYS)] for way in range(WAYS))
        each(0, WAYS, codes_on)
        each(1, WAYS, rows)
        regroup(q)
        each(0, WAYS, rows_on)

    each(SPLIT, CHUNKS, pass_late)

    load_cent.wait()

    def norms(i):
        rows = pl.ds(pl.multiple_of(i * 32, 32), 32)
        wide = cent[rows, :].astype(F32)
        half_norm[rows, :] = 0.5 * jnp.sum(wide * wide, axis=1, keepdims=True)

    each(0, MESO_DEV * KF // 32, norms)

    def clear(i):
        rows = pl.ds(pl.multiple_of(i * 32, 32), 32)
        sums[rows, :] = jnp.zeros((32, D), F32)

    each(0, MESO_DEV * FGROUP // 32, clear)
    counts[...] = jnp.zeros_like(counts)
    msum[...] = jnp.zeros_like(msum)
    mcount[...] = jnp.zeros_like(mcount)

    def codes_from(tile, hit, pick):
        tile = tile.astype(I32)
        high = dot((tile >> 4).astype(F32).astype(BF16), pick)
        low = dot((tile & 15).astype(F32).astype(BF16), pick)
        high = jnp.sum(jnp.where(hit, high, 0.0), axis=0, keepdims=True)
        low = jnp.sum(jnp.where(hit, low, 0.0), axis=0, keepdims=True)
        return (high.astype(I32) - 1, low.astype(I32))

    def add_meso(members, high):
        hot = (iota((MESO_DEV, members.shape[0]), 0) == high).astype(F32)
        msum[...] += dot(hot.astype(BF16), members)
        mcount[...] += jnp.sum(hot, axis=1, keepdims=True)

    def nearest(members, high):
        size = members.shape[0]
        step = LANES if size % LANES == 0 else size
        eye = iota((step, step), 0) == iota((step, step), 1)
        norm = jnp.concatenate(
            [
                jnp.sum(
                    jnp.where(eye, dot(members[t : t + step], members[t : t + step], NT), 0.0), axis=0, keepdims=True
                )
                for t in range(0, size, step)
            ],
            axis=1,
        )

        best = jnp.zeros((1, size), F32)
        for i in range(0, MESO_DEV * KF, 1024):
            cross = dot(cent[i : i + 1024, :], members, NT) - half_norm[i : i + 1024, :]
            for t in range(0, 1024, KF):
                top = jnp.max(cross[t : t + KF], axis=0, keepdims=True)
                best = jnp.where(high == (i + t) // KF, top, best)
        return jnp.where(high >= 0, (norm - 2.0 * best) * (1.0 / D), 0.0)

    def add_fine(members, high, low):
        code = (high << 4) + low
        size = members.shape[0]

        def step(i):
            rows = pl.ds(pl.multiple_of(i * 128, 128), 128)
            hot = (iota((128, size), 0) + i * 128 == code).astype(F32)
            sums[rows, :] += dot(hot.astype(BF16), members)
            counts[rows, :] += jnp.sum(hot, axis=1, keepdims=True)

        each(0, MESO_DEV * FGROUP // 128, step)

    def spread_of(near, hit, pick):
        return sum(dot(piece, pick, NT) for piece in split3(jnp.where(hit, near, 0.0)))

    def pass_on(q):
        def codes(way):
            at = q * WAYS + way
            arrived(code1_got.at[at], c1_send.at[at], c1_recv.at[at])

        def rows(way):
            at = q * WAYS + way
            arrived(got1.at[q, block(way)], s1_send.at[at], s1_recv.at[at])

        def codes_on(way):
            at = q * WAYS + way
            link(code1_got.at[ways(q)], code2.at[ways(at)], c2_send.at[at], c2_recv.at[at], xc_peer(way)).start()

        def rows_on(way):
            at = q * WAYS + way
            link(mid.at[q, block(way)], got2.at[q, block(way)], s2_send.at[at], s2_recv.at[at], xc_peer(way)).start()

        each(start_of(q), WAYS, codes)
        code2[ways(q * WAYS)] = code1_got[ways(q)]
        each(1, WAYS, codes_on)
        each(start_of(q), WAYS, rows)
        regroup(q)
        got2[q, 0:BLOCK, :] = mid[q, 0:BLOCK, :]
        each(1, WAYS, rows_on)

    def work(q):
        def codes(way):
            at = q * WAYS + way
            arrived(code2.at[ways(at)], c2_send.at[at], c2_recv.at[at])

        def rows(way):
            at = q * WAYS + way
            arrived(got2.at[q, block(way)], s2_send.at[at], s2_recv.at[at])

        row = iota((LANES, CHUNK_ROWS), 1)
        pick = (iota((LANES, CHUNK_ROWS), 0) == div48(row) * SLOTS + row - 6 * div6(row)).astype(F32).astype(BF16)
        hit = iota((WAYS * WAYS, CHUNK_ROWS), 0) == div6(iota((WAYS * WAYS, CHUNK_ROWS), 1))
        each(1, WAYS, codes)
        tile = code2[pl.ds(q * WAYS * WAYS, WAYS * WAYS)].reshape(WAYS * WAYS, LANES)
        high, low = codes_from(tile, hit, pick)
        each(1, WAYS, rows)
        members = got2[q]
        spread = spread_of(nearest(members, high), hit, pick)
        for r in range(WAYS * WAYS):
            ret1[q * WAYS * WAYS + r] = spread[r : r + 1, :]
        ret1_got[ways(q * WAYS)] = ret1[ways(q * WAYS)]

        def back(way):
            at = q * WAYS + way
            link(ret1.at[ways(at)], ret1_got.at[ways(at)], r1_send.at[at], r1_recv.at[at], xc_back(way)).start()

        each(1, WAYS, back)
        add_meso(members, high)
        add_fine(members, high, low)

    def pass_back(q):
        def wait(way):
            at = q * WAYS + way
            arrived(ret1_got.at[ways(at)], r1_send.at[at], r1_recv.at[at])

        def back(way):
            at = q * WAYS + way
            link(ret_mid.at[at], ret2.at[at], r2_send.at[at], r2_recv.at[at], yz_back(q, way)).start()

        each(1, WAYS, wait)
        ret_mid[ways(q)] = sum(ret1_got[pl.ds((q * WAYS + way) * WAYS, WAYS)] for way in range(WAYS))
        each(start_of(q), WAYS, back)

    def turn(i):
        pass_on(i)

        @pl.when(i > 0)
        def _():
            pass_back(i - 1)

        work(i)

    each(0, SPLIT, turn)
    load_old.wait()

    def late_codes(at):
        arrived(last2.at[at], c2_send.at[EARLY + at], c2_recv.at[EARLY + at])

    def late_half(n):
        q = SPLIT + lax.div(n, 2)
        h = lax.rem(n, 2)
        late = lax.div(n, 2)
        row = iota((LANES, HALF), 1) + h * HALF
        pick = (iota((LANES, HALF), 0) == row - 48 * div48(row)).astype(F32).astype(BF16)
        hit = iota((WAYS, HALF), 0) == div48(iota((WAYS, HALF), 1) + h * HALF)

        @pl.when(h == 0)
        def _():
            each(late * WAYS, late * WAYS + WAYS, late_codes)

        high, low = codes_from(last2[ways(late)].reshape(WAYS, LANES), hit, pick)

        def rows(way):
            at = q * WAYS + way
            arrived(got2.at[q, block(way)], s2_send.at[at], s2_recv.at[at])

        start = h * (WAYS // 2)
        each(start, start + WAYS // 2, rows)
        members = got2[q, pl.ds(pl.multiple_of(h * HALF, HALF), HALF), :]
        add_meso(members, high)

        @pl.when(n == 2 * LATE - 1)
        def _():
            part[:, 0:D] = msum[...]
            part[:, D : D + LANES] = jnp.broadcast_to(mcount[...], (MESO_DEV, LANES))

            def share_out(dx):
                share = pl.ds(pl.multiple_of(lax.rem(x + dx, NX) * SHARE, SHARE), SHARE)
                device = xc_peer(dx * NC)
                link(part.at[share], part_got.at[dx - 1], p_send.at[dx - 1], p_recv.at[dx - 1], device).start()

            each(1, NX, share_out)

        spread = spread_of(nearest(members, high), hit, pick)
        for r in range(WAYS):
            @pl.when(h == r // (WAYS // 2))
            def _():
                back1[late * WAYS + r] = spread[r : r + 1, :]

        def back(way):
            at = late * WAYS + way
            device = yz_back(q, near_z(way))
            link(back1.at[at], back1_got.at[at], r1_send.at[EARLY + at], r1_recv.at[EARLY + at], device).start()

        each(start, start + WAYS // 2, back)
        add_fine(members, high, low)

        @pl.when(n == 1)
        def _():
            pass_back(SPLIT - 1)

    each(0, 2 * LATE, late_half)
    ret2[0] = ret_mid[0]

    def begin(m):
        rows = pl.ds(pl.multiple_of(m * FGROUP, FGROUP), FGROUP)
        mine = pl.ds(pl.multiple_of(m * KF + x * FGROUP, FGROUP), FGROUP)
        sums[rows, :] += cent[mine, :].astype(F32) - old[pl.ds(m, 1), :]

    each(0, MESO_DEV, begin)

    each(1, NX, lambda dx: arrived(part_got.at[dx - 1], p_send.at[dx - 1], p_recv.at[dx - 1]))
    share = pl.ds(pl.multiple_of(x * SHARE, SHARE), SHARE)
    total = (part[share, :] + part_got[1]) + (part_got[0] + part_got[2])
    new_part[...] = (total[:, 0:D] + old[share, :]) / (total[:, D : D + 1] + 1.0)

    def hand_out(dx):
        link(new_part, new_all.at[dx - 1], n_send.at[dx - 1], n_recv.at[dx - 1], xc_peer(dx * NC)).start()

    each(1, NX, hand_out)
    new_meso_ref[share, :] = new_part[...]

    def late_back(late):
        def wait(way):
            at = late * WAYS + way
            arrived(back1_got.at[at], r1_send.at[EARLY + at], r1_recv.at[EARLY + at])

        def back(way):
            at = late * WAYS + way
            link(
                back1_got.at[ways(late)], ret2.at[pl.ds(EARLY + at * WAYS, WAYS)], r2_send.at[EARLY + at], r2_recv.at[EARLY + at], xc_back(way)
            ).start()

        each(0, WAYS, wait)
        ret2[pl.ds(EARLY + late * PAIRS, WAYS)] = back1_got[ways(late)]
        each(1, WAYS, back)

    each(0, LATE, late_back)

    for dx in range(1, NX):
        arrived(new_all.at[dx - 1], n_send.at[dx - 1], n_recv.at[dx - 1])
        share = pl.ds(pl.multiple_of(lax.rem(x + NX - dx, NX) * SHARE, SHARE), SHARE)
        new_meso_ref[share, :] = new_all[dx - 1]

    def finish(m):
        rows = pl.ds(pl.multiple_of(m * FGROUP, FGROUP), FGROUP)
        new_fine_ref[rows, :] = (sums[rows, :] + new_meso_ref[pl.ds(m, 1), :]) / (counts[rows, :] + 1.0)

    each(0, MESO_DEV, finish)

    from_row = jnp.where(is_last, bin_of - SPLIT * PAIRS + EARLY, first)
    row_hot = (iota((EARLY + LATE * PAIRS, ROWS), 0) == from_row).astype(F32).astype(BF16)
    mine = iota((LANES, ROWS), 0) == jnp.where(is_last, hop1, hop2) * SLOTS + rank
    each(1, EARLY, lambda at: arrived(ret2.at[at], r2_send.at[at], r2_recv.at[at]))

    def late_returned(n):
        late = lax.div(n, WAYS - 1)
        at = late * WAYS + 1 + lax.rem(n, WAYS - 1)
        arrived(ret2.at[pl.ds(EARLY + at * WAYS, WAYS)], r2_send.at[EARLY + at], r2_recv.at[EARLY + at])

    each(0, LATE * (WAYS - 1), late_returned)
    returned = ret2[...].reshape(EARLY + LATE * PAIRS, LANES)
    picked = sum(dot(piece, row_hot, TN) for piece in split3(returned))
    near_ref[...] = jnp.sum(jnp.where(mine, picked, 0.0), axis=0, keepdims=True).reshape(ROWS)

    def early_left(at):
        q = lax.div(at, WAYS)
        way = lax.rem(at, WAYS)
        left(packed.at[q, block(way)], s1_send.at[at], s1_recv.at[at])
        left(code1.at[at], c1_send.at[at], c1_recv.at[at])
        left(ret_mid.at[at], r2_send.at[at], r2_recv.at[at])

    def early_left2(at):
        q = lax.div(at, WAYS - 1)
        way = lax.rem(at, WAYS - 1) + 1
        at = q * WAYS + way
        left(mid.at[q, block(way)], s2_send.at[at], s2_recv.at[at])
        left(code1_got.at[ways(q)], c2_send.at[at], c2_recv.at[at])
        left(ret1.at[ways(at)], r1_send.at[at], r1_recv.at[at])

    def late_left(n):
        late = lax.div(n, WAYS - 1)
        way = lax.rem(n, WAYS - 1) + 1
        at = EARLY + late * WAYS + way
        left(packed.at[SPLIT + late, block(way)], s1_send.at[at], s1_recv.at[at])
        left(last1.at[ways(late * WAYS + way)], c1_send.at[at], c1_recv.at[at])
        left(back1_got.at[ways(late)], r2_send.at[at], r2_recv.at[at])

    def late_left2(n):
        late = lax.div(n, WAYS)
        way = lax.rem(n, WAYS)
        at = EARLY + n
        left(mid.at[SPLIT + late, block(way)], s2_send.at[at], s2_recv.at[at])
        left(last_mid.at[n], c2_send.at[at], c2_recv.at[at])
        left(back1.at[n], r1_send.at[at], r1_recv.at[at])

    def meso_left(dx):
        left(part_got.at[dx], p_send.at[dx], p_recv.at[dx])
        left(new_part, n_send.at[dx], n_recv.at[dx])

    each(1, EARLY, early_left)
    each(0, SPLIT * (WAYS - 1), early_left2)
    each(0, LATE * (WAYS - 1), late_left)
    each(0, LATER, late_left2)
    each(0, NX - 1, meso_left)


def body(vectors, meso_labels, fine_labels, meso_centroids, fine_centroids):
    hbm = pl.BlockSpec(memory_space=pl.ANY)
    vmem = pl.BlockSpec(memory_space=pltpu.VMEM)
    hops = CHUNKS * WAYS
    dma = pltpu.SemaphoreType.DMA
    outs = (((ROWS,), F32), ((MESO_DEV, D), F32), ((MESO_DEV * FGROUP, D), F32))

    def row(count):
        return pltpu.VMEM((count, 1, LANES), F32)

    near, new_meso, new_fine = pl.pallas_call(
        kernel,
        out_shape=tuple(pltpu.VMEM(*out) for out in outs),
        in_specs=[hbm] * 5,
        out_specs=(vmem,) * 3,
        scratch_shapes=[
            pltpu.VMEM((ROWS,), I32),
            pltpu.VMEM((ROWS,), I32),
            pltpu.VMEM((ROWS, D), BF16),
            pltpu.VMEM((MESO_DEV, D), F32),
            pltpu.VMEM((MESO_DEV * KF, D), BF16),
            pltpu.VMEM((MESO_DEV * KF, 1), F32),
            pltpu.VMEM((CHUNK_ROWS, CHUNK_ROWS), BF16),
            pltpu.VMEM((CHUNKS, CHUNK_ROWS, D), BF16),
            pltpu.VMEM((CHUNKS, CHUNK_ROWS, D), BF16),
            pltpu.VMEM((CHUNKS, CHUNK_ROWS, D), BF16),
            pltpu.VMEM((CHUNKS, CHUNK_ROWS, D), BF16),
            row(EARLY), row(EARLY), row(EARLY * WAYS),
            row(LATE * PAIRS), row(LATE * PAIRS), row(LATER), row(LATER),
            row(EARLY * WAYS), row(EARLY * WAYS), row(EARLY),
            row(LATER), row(LATER), row(EARLY + LATE * PAIRS),
            pltpu.VMEM((MESO_DEV * FGROUP, D), F32),
            pltpu.VMEM((MESO_DEV * FGROUP, 1), F32),
            pltpu.VMEM((MESO_DEV, D), F32),
            pltpu.VMEM((MESO_DEV, 1), F32),
            pltpu.VMEM((MESO_DEV, D + LANES), F32),
            pltpu.VMEM((NX - 1, SHARE, D + LANES), F32),
            pltpu.VMEM((SHARE, D), F32),
            pltpu.VMEM((NX - 1, SHARE, D), F32),
            pltpu.VMEM((CHUNK_ROWS, ROWS), BF16),
            pltpu.VMEM((BINS, ROWS), BF16),
            pltpu.VMEM((1, ROWS), I32),
            pltpu.VMEM((1, ROWS), I32),
            pltpu.VMEM((1, ROWS), I32),
            dma((5,)),
        ]
        + [dma((hops,)) for _ in range(12)]
        + [dma((NX - 1,)) for _ in range(4)]
        + [pltpu.SemaphoreType.REGULAR],
        compiler_params=pltpu.CompilerParams(
            collective_id=0, has_side_effects=True, vmem_limit_bytes=61 * 2**20
        ),
    )(
        meso_labels,
        fine_labels,
        vectors,
        meso_centroids,
        fine_centroids.reshape(MESO_DEV * KF, D),
    )
    return (near, new_meso, new_fine.reshape(MESO_DEV, FGROUP, D))


def solution(mesh):
    return jax.shard_map(
        body,
        mesh=mesh,
        in_specs=(
            P(("dp", "owner"), None),
            P(("dp", "owner")),
            P(("dp", "owner")),
            P("owner", None),
            P("owner", None, None),
        ),
        out_specs=(P(("dp", "owner")), P("owner", None), P("owner", "dp", None)),
        check_vma=False,
    )
```

```python
import jax
import jax.numpy as jnp
from jax import lax
from jax.experimental import pallas as pl
from jax.experimental.pallas import tpu as pltpu
from jax.sharding import PartitionSpec as P

MESH = pl.DeviceIdType.MESH
D = 1024
ROWS = 768
KF = 64
MESO_DEV = 32
FGROUP = 16
SLOTS = 6
NX, NY, NZ, NC = 4, 4, 8, 2
CHUNKS = NY
WAYS = 8
BLOCK = WAYS * SLOTS
CHUNK_ROWS = WAYS * BLOCK
BINS = CHUNKS * WAYS * WAYS
LANES = 128
SHARE = MESO_DEV // NX
SPLIT = 2
LATE = CHUNKS - SPLIT
EARLY = SPLIT * WAYS
LATER = LATE * WAYS
PAIRS = WAYS * WAYS
HALF = CHUNK_ROWS // 2

F32, BF16, I32 = jnp.float32, jnp.bfloat16, jnp.int32
NT = (((1,), (1,)), ((), ()))
TN = (((0,), (0,)), ((), ()))


def iota(shape, dim):
    return lax.broadcasted_iota(I32, shape, dim)


def div6(v):
    return (v * 10923) >> 16


def div48(v):
    return div6(v >> 3)


def split3(v):
    first = v.astype(BF16)
    rest = v - first.astype(F32)
    second = rest.astype(BF16)
    third = (rest - second.astype(F32)).astype(BF16)
    return (first, second, third)


def dot(a, b, dims=(((1,), (0,)), ((), ()))):
    return lax.dot_general(a, b, dims, preferred_element_type=F32)


def each(low, high, step):
    def body(i, carry):
        step(i)
        return carry

    lax.fori_loop(low, high, body, 0)


def kernel(
    meso_hbm, fine_hbm, vec_hbm, old_hbm, cent_hbm,
    near_ref, new_meso_ref, new_fine_ref,
    meso_ref, fine_ref, vec, old, cent, half_norm, perm, packed, got1, mid, got2,
    code1, code1_got, code2, last1, last1_got, last_mid, last2,
    ret1, ret1_got, ret_mid, back1, ret2,
    sums, counts, msum, mcount, part, part_got, new_part, new_all,
    hot_ref, bin_hot, bin_ref, rank_ref, slot_ref, row_hot, inverse,
    load_sem, s1_send, s1_recv, s2_send, s2_recv, c1_send, c1_recv, c2_send, c2_recv,
    r1_send, r1_recv, r2_send, r2_recv, p_send, p_recv, n_send, n_recv, gate,
):
    x = lax.axis_index("dp")
    own = lax.axis_index("owner")
    y, z, c = lax.div(own, 16), lax.rem(lax.div(own, 2), 8), lax.rem(own, 2)

    def yz_peer(dy, dz):
        return (x, (lax.rem(y + dy, NY) * NZ + lax.rem(z + dz, NZ)) * NC + c)

    def xc_peer(j):
        return (lax.rem(x + lax.div(j, NC), NX), (y * NZ + z) * NC + lax.rem(c + lax.rem(j, NC), NC))

    def xc_back(j):
        return (lax.rem(x + NX - lax.div(j, NC), NX), (y * NZ + z) * NC + lax.rem(c + lax.rem(j, NC), NC))

    def yz_back(dy, dz):
        return yz_peer(NY - dy, NZ - dz)

    def near_z(way):
        odd = lax.rem(way, 2)
        return lax.rem(odd * lax.div(way + 1, 2) + (1 - odd) * lax.div(2 * NZ - way, 2), NZ)

    def start_of(q):
        return lax.div(SPLIT - q, SPLIT)

    def link(src, dst, send_sem, recv_sem, device):
        return pltpu.make_async_remote_copy(
            src_ref=src, dst_ref=dst, send_sem=send_sem, recv_sem=recv_sem,
            device_id=device, device_id_type=MESH,
        )

    here = (x, own)

    def arrived(dst, send_sem, recv_sem):
        link(dst, dst, send_sem, recv_sem, here).wait_recv()

    def left(src, send_sem, recv_sem):
        link(src, src, send_sem, recv_sem, here).wait_send()

    def block(way):
        return pl.ds(pl.multiple_of(way * BLOCK, BLOCK), BLOCK)

    def ways(at):
        return pl.ds(at * WAYS, WAYS)

    barrier = pltpu.get_barrier_semaphore()

    def greet(device):
        pl.semaphore_signal(barrier, 1, device_id=device, device_id_type=MESH)

    each(1, NZ, lambda dz: greet(yz_peer(0, dz)))
    each(1, NY, lambda dy: greet(yz_peer(dy, 0)))
    each(1, WAYS, lambda j: greet(xc_peer(j)))
    greeted = NZ + NY + WAYS - 3

    load_meso = pltpu.make_async_copy(meso_hbm, meso_ref, load_sem.at[3])
    load_fine = pltpu.make_async_copy(fine_hbm, fine_ref, load_sem.at[4])
    load_vec = pltpu.make_async_copy(vec_hbm, vec, load_sem.at[0])
    load_cent = pltpu.make_async_copy(cent_hbm, cent, load_sem.at[1])
    load_old = pltpu.make_async_copy(old_hbm, old, load_sem.at[2])
    for load in (load_meso, load_fine, load_vec, load_cent, load_old):
        load.start()

    load_meso.wait()
    load_fine.wait()
    meso = meso_ref[...].reshape(1, ROWS)
    fine = fine_ref[...].reshape(1, ROWS)
    to = meso >> 5
    dy = ((to >> 4) - y) & 3
    dz = (((to >> 1) & 7) - z) & 7
    way = ((((fine >> 4) - x) & 3) << 1) + ((to - c) & 1)
    z_near = jnp.where(dz <= 4, jnp.maximum(2 * dz - 1, 0), 2 * (NZ - dz))
    is_last = dy >= SPLIT
    hop1 = jnp.where(is_last, way, dz)
    hop2 = jnp.where(is_last, z_near, way)
    first = (dy << 3) + hop1
    bin_of = (first << 3) + hop2
    bin_ref[...] = bin_of

    def bin_rows(i):
        rows = pl.ds(pl.multiple_of(i * 64, 64), 64)
        bin_hot[rows, :] = (iota((64, ROWS), 0) + i * 64 == bin_of).astype(F32).astype(BF16)

    each(0, BINS // 64, bin_rows)

    def ranks(i):
        lanes = pl.ds(pl.multiple_of(i * LANES, LANES), LANES)
        before = (iota((ROWS, LANES), 0) < iota((ROWS, LANES), 1) + i * LANES).astype(F32).astype(BF16)
        ahead = dot(bin_hot[...], before)
        mine = iota((BINS, LANES), 0) == bin_ref[:, lanes]
        rank_ref[:, lanes] = jnp.sum(jnp.where(mine, ahead, 0.0), axis=0, keepdims=True).astype(I32)

    each(0, ROWS // LANES, ranks)
    rank = rank_ref[...]
    slot_ref[...] = bin_of * SLOTS + rank

    meso_code = ((meso & 31) + 1).astype(F32)
    fine_code = (fine & 15).astype(F32)

    def code_rows(hit, lane):
        hot = (iota((LANES, ROWS), 0) == lane).astype(F32).astype(BF16)
        high = jnp.where(hit, meso_code, 0.0).astype(BF16)
        low = jnp.where(hit, fine_code, 0.0).astype(BF16)
        return 16.0 * dot(high, hot, NT) + dot(low, hot, NT)

    codes = code_rows(iota((EARLY, ROWS), 0) == first, hop2 * SLOTS + rank)
    for r in range(EARLY):
        code1[r] = codes[r : r + 1, :]
    load_vec.wait()

    def pack(q):
        def hot_rows(i):
            rows = pl.ds(pl.multiple_of(i * 64, 64), 64)
            at = iota((64, ROWS), 0) + (q * CHUNK_ROWS + i * 64)
            hot_ref[rows, :] = (at == slot_ref[...]).astype(F32).astype(BF16)

        def columns(i):
            lanes = pl.ds(pl.multiple_of(i * 256, 256), 256)
            packed[q, :, lanes] = dot(hot_ref[...], vec[:, lanes]).astype(BF16)

        each(0, CHUNK_ROWS // 64, hot_rows)
        each(0, D // 256, columns)

    def leave_late(q):
        late = q - SPLIT

        def code(way):
            at = ways(late * WAYS + way)
            link(last1.at[at], last1_got.at[at], c1_send.at[q], c1_recv.at[q], xc_peer(way)).start()

        def rows(way):
            link(packed.at[q, block(way)], got1.at[q, block(way)], s1_send.at[q], s1_recv.at[q], xc_peer(way)).start()

        pack(q)
        last1_got[ways(late * WAYS)] = last1[ways(late * WAYS)]
        got1[q, 0:BLOCK, :] = packed[q, 0:BLOCK, :]
        each(1, WAYS, code)
        each(1, WAYS, rows)

    def leave_early(q):
        def code(way):
            at = q * WAYS + way
            link(code1.at[at], code1_got.at[at], c1_send.at[q], c1_recv.at[q], yz_peer(q, way)).start()

        def rows(way):
            link(packed.at[q, block(way)], got1.at[q, block(way)], s1_send.at[q], s1_recv.at[q], yz_peer(q, way)).start()

        each(start_of(q), WAYS, code)
        each(start_of(q), WAYS, rows)

    def signal(dy):
        pl.semaphore_signal(gate, 1, device_id=yz_peer(dy, 0), device_id_type=MESH)

    pack(0)
    code1_got[0] = code1[0]
    got1[0, 0:BLOCK, :] = packed[0, 0:BLOCK, :]
    pl.semaphore_wait(barrier, greeted)
    leave_early(0)
    each(1, NY, signal)
    codes = code_rows(iota((LATE * PAIRS, ROWS), 0) + SPLIT * PAIRS == bin_of, hop1 * SLOTS + rank)
    for r in range(LATE * PAIRS):
        last1[r] = codes[r : r + 1, :]
    each(SPLIT, CHUNKS, leave_late)
    each(1, SPLIT, pack)
    pl.semaphore_wait(gate, NY - 1)
    each(1, SPLIT, leave_early)

    def perm_rows(i):
        rows = pl.ds(pl.multiple_of(i * 64, 64), 64)
        out_row = iota((64, CHUNK_ROWS), 0) + i * 64
        in_row = iota((64, CHUNK_ROWS), 1)
        out_pair, in_pair = div6(out_row), div6(in_row)
        swapped = ((out_pair & 7) << 3) + (out_pair >> 3)
        hit = in_row - 6 * in_pair + 6 * swapped == out_row - 6 * out_pair + 6 * in_pair
        perm[rows, :] = hit.astype(F32).astype(BF16)

    each(0, CHUNK_ROWS // 64, perm_rows)

    def regroup(q):
        def columns(i):
            lanes = pl.ds(pl.multiple_of(i * 256, 256), 256)
            mid[q, :, lanes] = dot(perm[...], got1[q, :, lanes]).astype(BF16)

        each(0, D // 256, columns)

    def pass_late(q):
        late = q - SPLIT

        def codes_on(way):
            at = late * WAYS + way
            link(last_mid.at[at], last2.at[at], c2_send.at[q], c2_recv.at[q], yz_peer(q, near_z(way))).start()

        def rows_on(way):
            half = s2_recv.at[SPLIT + late * 2 + lax.div(way, WAYS // 2)]
            link(mid.at[q, block(way)], got2.at[q, block(way)], s2_send.at[q], half, yz_peer(q, near_z(way))).start()

        arrived(last1_got.at[pl.ds(late * PAIRS + WAYS, PAIRS - WAYS)], c1_send.at[q], c1_recv.at[q])
        last_mid[ways(late)] = sum(last1_got[pl.ds(late * PAIRS + way * WAYS, WAYS)] for way in range(WAYS))
        each(0, WAYS, codes_on)
        arrived(got1.at[q, pl.ds(BLOCK, CHUNK_ROWS - BLOCK)], s1_send.at[q], s1_recv.at[q])
        regroup(q)
        each(0, WAYS, rows_on)

    each(SPLIT, CHUNKS, pass_late)

    load_cent.wait()

    def norms(i):
        rows = pl.ds(pl.multiple_of(i * 32, 32), 32)
        wide = cent[rows, :].astype(F32)
        half_norm[rows, :] = 0.5 * jnp.sum(wide * wide, axis=1, keepdims=True)

    each(0, MESO_DEV * KF // 32, norms)

    load_old.wait()

    def begin(m):
        rows = pl.ds(pl.multiple_of(m * FGROUP, FGROUP), FGROUP)
        mine = pl.ds(pl.multiple_of(m * KF + x * FGROUP, FGROUP), FGROUP)
        sums[rows, :] = cent[mine, :].astype(F32) - old[pl.ds(m, 1), :]

    each(0, MESO_DEV, begin)
    from_row = jnp.where(is_last, bin_of - SPLIT * PAIRS + EARLY, first)

    def from_rows(i):
        rows = pl.ds(pl.multiple_of(i * 16, 16), 16)
        row_hot[rows, :] = (iota((16, ROWS), 0) + i * 16 == from_row).astype(F32).astype(BF16)

    each(0, (EARLY + LATE * PAIRS) // 16, from_rows)
    counts[...] = jnp.zeros_like(counts)
    msum[...] = jnp.zeros_like(msum)
    mcount[...] = jnp.zeros_like(mcount)

    def codes_from(tile, hit, pick):
        tile = tile.astype(I32)
        high = dot((tile >> 4).astype(F32).astype(BF16), pick)
        low = dot((tile & 15).astype(F32).astype(BF16), pick)
        high = jnp.sum(jnp.where(hit, high, 0.0), axis=0, keepdims=True)
        low = jnp.sum(jnp.where(hit, low, 0.0), axis=0, keepdims=True)
        return (high.astype(I32) - 1, low.astype(I32))

    def add_meso(members, high):
        hot = (iota((MESO_DEV, members.shape[0]), 0) == high).astype(F32)
        msum[...] += dot(hot.astype(BF16), members)
        mcount[...] += jnp.sum(hot, axis=1, keepdims=True)

    def nearest(members, high):
        size = members.shape[0]
        step = LANES if size % LANES == 0 else size
        eye = iota((step, step), 0) == iota((step, step), 1)
        norm = jnp.concatenate(
            [
                jnp.sum(
                    jnp.where(eye, dot(members[t : t + step], members[t : t + step], NT), 0.0), axis=0, keepdims=True
                )
                for t in range(0, size, step)
            ],
            axis=1,
        )

        best = jnp.zeros((1, size), F32)
        for i in range(0, MESO_DEV * KF, 1024):
            cross = dot(cent[i : i + 1024, :], members, NT) - half_norm[i : i + 1024, :]
            for t in range(0, 1024, KF):
                top = jnp.max(cross[t : t + KF], axis=0, keepdims=True)
                best = jnp.where(high == (i + t) // KF, top, best)
        return jnp.where(high >= 0, (norm - 2.0 * best) * (1.0 / D), 0.0)

    def add_fine(members, high, low):
        code = (high << 4) + low
        size = members.shape[0]

        def step(i):
            rows = pl.ds(pl.multiple_of(i * 128, 128), 128)
            hot = (iota((128, size), 0) + i * 128 == code).astype(F32)
            sums[rows, :] += dot(hot.astype(BF16), members)
            counts[rows, :] += jnp.sum(hot, axis=1, keepdims=True)

        each(0, MESO_DEV * FGROUP // 128, step)

    def spread_of(near, hit, pick):
        return sum(dot(piece, pick, NT) for piece in split3(jnp.where(hit, near, 0.0)))

    def early_rows(step, q, ref, send_sem, recv_sem):
        @pl.when(q == 0)
        def _():
            step(ref(1), send_sem, recv_sem)

        @pl.when(q > 0)
        def _():
            step(ref(0), send_sem, recv_sem)

    def tail_of(ref, q):
        return lambda way: ref.at[pl.ds(q * WAYS + way, WAYS - way)]

    def rows_of(ref, q):
        return lambda way: ref.at[q, pl.ds(way * BLOCK, CHUNK_ROWS - way * BLOCK)]

    def tiles_of(ref, q):
        return ref.at[pl.ds(q * PAIRS + WAYS, PAIRS - WAYS)]

    def pass_on(q):
        def codes_on(way):
            at = q * WAYS + way
            link(code1_got.at[ways(q)], code2.at[ways(at)], c2_send.at[q], c2_recv.at[q], xc_peer(way)).start()

        def rows_on(way):
            link(mid.at[q, block(way)], got2.at[q, block(way)], s2_send.at[q], s2_recv.at[q], xc_peer(way)).start()

        early_rows(arrived, q, tail_of(code1_got, q), c1_send.at[q], c1_recv.at[q])
        code2[ways(q * WAYS)] = code1_got[ways(q)]
        each(1, WAYS, codes_on)
        early_rows(arrived, q, rows_of(got1, q), s1_send.at[q], s1_recv.at[q])
        regroup(q)
        got2[q, 0:BLOCK, :] = mid[q, 0:BLOCK, :]
        each(1, WAYS, rows_on)

    def work(q):
        row = iota((LANES, CHUNK_ROWS), 1)
        pick = (iota((LANES, CHUNK_ROWS), 0) == div48(row) * SLOTS + row - 6 * div6(row)).astype(F32).astype(BF16)
        hit = iota((WAYS * WAYS, CHUNK_ROWS), 0) == div6(iota((WAYS * WAYS, CHUNK_ROWS), 1))
        arrived(tiles_of(code2, q), c2_send.at[q], c2_recv.at[q])
        tile = code2[pl.ds(q * PAIRS, PAIRS)].reshape(PAIRS, LANES)
        high, low = codes_from(tile, hit, pick)
        arrived(got2.at[q, pl.ds(BLOCK, CHUNK_ROWS - BLOCK)], s2_send.at[q], s2_recv.at[q])
        members = got2[q]
        spread = spread_of(nearest(members, high), hit, pick)
        for r in range(PAIRS):
            ret1[q * PAIRS + r] = spread[r : r + 1, :]
        ret1_got[ways(q * WAYS)] = ret1[ways(q * WAYS)]

        def back(way):
            at = ways(q * WAYS + way)
            link(ret1.at[at], ret1_got.at[at], r1_send.at[q], r1_recv.at[q], xc_back(way)).start()

        each(1, WAYS, back)
        add_meso(members, high)
        add_fine(members, high, low)

    def pass_back(q):
        def back(way):
            at = q * WAYS + way
            link(ret_mid.at[at], ret2.at[at], r2_send.at[q], r2_recv.at[q], yz_back(q, way)).start()

        arrived(tiles_of(ret1_got, q), r1_send.at[q], r1_recv.at[q])
        ret_mid[ways(q)] = sum(ret1_got[pl.ds((q * WAYS + way) * WAYS, WAYS)] for way in range(WAYS))
        each(start_of(q), WAYS, back)

    def turn(i):
        pass_on(i)

        @pl.when(i > 0)
        def _():
            pass_back(i - 1)

        work(i)

    each(0, SPLIT, turn)

    def early_left(q):
        early_rows(left, q, rows_of(packed, q), s1_send.at[q], s1_recv.at[q])
        early_rows(left, q, tail_of(code1, q), c1_send.at[q], c1_recv.at[q])
        left(mid.at[q, pl.ds(BLOCK, CHUNK_ROWS - BLOCK)], s2_send.at[q], s2_recv.at[q])
        left(tiles_of(code2, q), c2_send.at[q], c2_recv.at[q])
        left(tiles_of(ret1, q), r1_send.at[q], r1_recv.at[q])

    def late_left(q):
        left(packed.at[q, pl.ds(BLOCK, CHUNK_ROWS - BLOCK)], s1_send.at[q], s1_recv.at[q])
        left(tiles_of(last1, q - SPLIT), c1_send.at[q], c1_recv.at[q])

    def late_half(n):
        q = SPLIT + lax.div(n, 2)
        h = lax.rem(n, 2)
        late = lax.div(n, 2)
        row = iota((LANES, HALF), 1) + h * HALF
        pick = (iota((LANES, HALF), 0) == row - 48 * div48(row)).astype(F32).astype(BF16)
        hit = iota((WAYS, HALF), 0) == div48(iota((WAYS, HALF), 1) + h * HALF)

        @pl.when(h == 0)
        def _():
            arrived(last2.at[ways(late)], c2_send.at[q], c2_recv.at[q])

        high, low = codes_from(last2[ways(late)].reshape(WAYS, LANES), hit, pick)

        half = pl.ds(pl.multiple_of(h * HALF, HALF), HALF)
        arrived(got2.at[q, half], s2_send.at[q], s2_recv.at[SPLIT + n])
        members = got2[q, half, :]
        add_meso(members, high)

        @pl.when(n == 2 * LATE - 1)
        def _():
            part[:, 0:D] = msum[...]
            part[:, D : D + LANES] = jnp.broadcast_to(mcount[...], (MESO_DEV, LANES))

            def share_out(dx):
                share = pl.ds(pl.multiple_of(lax.rem(x + dx, NX) * SHARE, SHARE), SHARE)
                device = xc_peer(dx * NC)
                link(part.at[share], part_got.at[dx - 1], p_send, p_recv, device).start()

            each(1, NX, share_out)

        spread = spread_of(nearest(members, high), hit, pick)
        for r in range(WAYS):
            @pl.when(h == r // (WAYS // 2))
            def _():
                back1[late * WAYS + r] = spread[r : r + 1, :]

        def back(at):
            way = h * (WAYS // 2) + lax.div(at, WAYS)
            j = lax.rem(at, WAYS)
            row = late * WAYS + way
            to = EARLY + late * PAIRS + j * WAYS + way
            device = (
                lax.rem(x + NX - lax.div(j, NC), NX),
                (lax.rem(y + NY - q, NY) * NZ + lax.rem(z + NZ - near_z(way), NZ)) * NC + lax.rem(c + lax.rem(j, NC), NC),
            )
            link(back1.at[row], ret2.at[to], r2_send.at[q], r2_recv.at[q], device).start()

        each(0, PAIRS // 2, back)
        add_fine(members, high, low)

        @pl.when(n == 1)
        def _():
            pass_back(SPLIT - 1)
            each(0, SPLIT, early_left)
            each(SPLIT, CHUNKS, late_left)

    each(0, 2 * LATE, late_half)
    ret2[0] = ret_mid[0]

    inverse[...] = 1.0 / (counts[...] + 1.0)

    arrived(part_got, p_send, p_recv)
    share = pl.ds(pl.multiple_of(x * SHARE, SHARE), SHARE)
    total = (part[share, :] + part_got[1]) + (part_got[0] + part_got[2])
    new_part[...] = (total[:, 0:D] + old[share, :]) / (total[:, D : D + 1] + 1.0)

    def hand_out(dx):
        link(new_part, new_all.at[dx - 1], n_send, n_recv, xc_peer(dx * NC)).start()

    each(1, NX, hand_out)
    new_meso_ref[share, :] = new_part[...]

    arrived(new_all, n_send, n_recv)
    for dx in range(1, NX):
        share = pl.ds(pl.multiple_of(lax.rem(x + NX - dx, NX) * SHARE, SHARE), SHARE)
        new_meso_ref[share, :] = new_all[dx - 1]

    def finish(m):
        rows = pl.ds(pl.multiple_of(m * FGROUP, FGROUP), FGROUP)
        new_fine_ref[rows, :] = (sums[rows, :] + new_meso_ref[pl.ds(m, 1), :]) * inverse[rows, :]

    each(0, MESO_DEV, finish)

    mine = iota((LANES, ROWS), 0) == jnp.where(is_last, hop1, hop2) * SLOTS + rank
    arrived(ret2.at[pl.ds(1, WAYS - 1)], r2_send.at[0], r2_recv.at[0])
    for q in range(1, SPLIT):
        arrived(ret2.at[ways(q)], r2_send.at[q], r2_recv.at[q])
    for q in range(SPLIT, CHUNKS):
        arrived(ret2.at[pl.ds(EARLY + (q - SPLIT) * PAIRS, PAIRS)], r2_send.at[q], r2_recv.at[q])
    returned = ret2[...].reshape(EARLY + LATE * PAIRS, LANES)
    picked = sum(dot(piece, row_hot[...], TN) for piece in split3(returned))
    near_ref[...] = jnp.sum(jnp.where(mine, picked, 0.0), axis=0, keepdims=True).reshape(ROWS)

    left(code1.at[pl.ds(1, WAYS - 1)], r2_send.at[0], r2_recv.at[0])
    for q in range(1, SPLIT):
        left(code1.at[ways(q)], r2_send.at[q], r2_recv.at[q])
    for q in range(SPLIT, CHUNKS):
        left(mid.at[q], s2_send.at[q], s2_recv.at[q])
        left(last_mid.at[ways(q - SPLIT)], c2_send.at[q], c2_recv.at[q])
        left(last1.at[pl.ds((q - SPLIT) * PAIRS, PAIRS)], r2_send.at[q], r2_recv.at[q])
    left(part_got, p_send, p_recv)
    left(new_all, n_send, n_recv)


def body(vectors, meso_labels, fine_labels, meso_centroids, fine_centroids):
    hbm = pl.BlockSpec(memory_space=pl.ANY)
    vmem = pl.BlockSpec(memory_space=pltpu.VMEM)
    dma = pltpu.SemaphoreType.DMA
    outs = (((ROWS,), F32), ((MESO_DEV, D), F32), ((MESO_DEV * FGROUP, D), F32))

    def row(count):
        return pltpu.VMEM((count, 1, LANES), F32)

    near, new_meso, new_fine = pl.pallas_call(
        kernel,
        out_shape=tuple(pltpu.VMEM(*out) for out in outs),
        in_specs=[hbm] * 5,
        out_specs=(vmem,) * 3,
        scratch_shapes=[
            pltpu.VMEM((ROWS,), I32),
            pltpu.VMEM((ROWS,), I32),
            pltpu.VMEM((ROWS, D), BF16),
            pltpu.VMEM((MESO_DEV, D), F32),
            pltpu.VMEM((MESO_DEV * KF, D), BF16),
            pltpu.VMEM((MESO_DEV * KF, 1), F32),
            pltpu.VMEM((CHUNK_ROWS, CHUNK_ROWS), BF16),
            pltpu.VMEM((CHUNKS, CHUNK_ROWS, D), BF16),
            pltpu.VMEM((CHUNKS, CHUNK_ROWS, D), BF16),
            pltpu.VMEM((CHUNKS, CHUNK_ROWS, D), BF16),
            pltpu.VMEM((CHUNKS, CHUNK_ROWS, D), BF16),
            row(EARLY), row(EARLY), row(EARLY * WAYS),
            row(LATE * PAIRS), row(LATE * PAIRS), row(LATER), row(LATER),
            row(EARLY * WAYS), row(EARLY * WAYS), row(EARLY),
            row(LATER), row(EARLY + LATE * PAIRS),
            pltpu.VMEM((MESO_DEV * FGROUP, D), F32),
            pltpu.VMEM((MESO_DEV * FGROUP, 1), F32),
            pltpu.VMEM((MESO_DEV, D), F32),
            pltpu.VMEM((MESO_DEV, 1), F32),
            pltpu.VMEM((MESO_DEV, D + LANES), F32),
            pltpu.VMEM((NX - 1, SHARE, D + LANES), F32),
            pltpu.VMEM((SHARE, D), F32),
            pltpu.VMEM((NX - 1, SHARE, D), F32),
            pltpu.VMEM((CHUNK_ROWS, ROWS), BF16),
            pltpu.VMEM((BINS, ROWS), BF16),
            pltpu.VMEM((1, ROWS), I32),
            pltpu.VMEM((1, ROWS), I32),
            pltpu.VMEM((1, ROWS), I32),
            pltpu.VMEM((EARLY + LATE * PAIRS, ROWS), BF16),
            pltpu.VMEM((MESO_DEV * FGROUP, 1), F32),
            dma((5,)),
        ]
        + [dma((CHUNKS,)), dma((CHUNKS,)), dma((CHUNKS,)), dma((SPLIT + 2 * LATE,))]
        + [dma((CHUNKS,)) for _ in range(8)]
        + [dma] * 4
        + [pltpu.SemaphoreType.REGULAR],
        compiler_params=pltpu.CompilerParams(
            collective_id=0, has_side_effects=True, vmem_limit_bytes=61 * 2**20
        ),
    )(
        meso_labels,
        fine_labels,
        vectors,
        meso_centroids,
        fine_centroids.reshape(MESO_DEV * KF, D),
    )
    return (near, new_meso, new_fine.reshape(MESO_DEV, FGROUP, D))


def solution(mesh):
    return jax.shard_map(
        body,
        mesh=mesh,
        in_specs=(
            P(("dp", "owner"), None),
            P(("dp", "owner")),
            P(("dp", "owner")),
            P("owner", None),
            P("owner", None, None),
        ),
        out_specs=(P(("dp", "owner")), P("owner", None), P("owner", "dp", None)),
        check_vma=False,
    )
```

```python
import jax
import jax.numpy as jnp
from jax import lax
from jax.experimental import pallas as pl
from jax.experimental.pallas import tpu as pltpu
from jax.sharding import PartitionSpec as P

MESH = pl.DeviceIdType.MESH
D = 1024
ROWS = 768
KF = 64
MESO_DEV = 32
FGROUP = 16
SLOTS = 6
NX, NY, NZ, NC = 4, 4, 8, 2
CHUNKS = NY
WAYS = 8
BLOCK = WAYS * SLOTS
CHUNK_ROWS = WAYS * BLOCK
BINS = CHUNKS * WAYS * WAYS
LANES = 128
SHARE = MESO_DEV // NX
SPLIT = 2
LATE = CHUNKS - SPLIT
EARLY = SPLIT * WAYS
LATER = LATE * WAYS
PAIRS = WAYS * WAYS
HALF = CHUNK_ROWS // 2

F32, BF16, I32 = jnp.float32, jnp.bfloat16, jnp.int32
NT = (((1,), (1,)), ((), ()))
TN = (((0,), (0,)), ((), ()))


def iota(shape, dim):
    return lax.broadcasted_iota(I32, shape, dim)


def div6(v):
    return (v * 10923) >> 16


def div48(v):
    return div6(v >> 3)


def split3(v):
    first = v.astype(BF16)
    rest = v - first.astype(F32)
    second = rest.astype(BF16)
    third = (rest - second.astype(F32)).astype(BF16)
    return (first, second, third)


def dot(a, b, dims=(((1,), (0,)), ((), ()))):
    return lax.dot_general(a, b, dims, preferred_element_type=F32)


def each(low, high, step):
    def body(i, carry):
        step(i)
        return carry

    lax.fori_loop(low, high, body, 0)


def kernel(
    meso_hbm, fine_hbm, vec_hbm, old_hbm, cent_hbm,
    near_ref, new_meso_ref, new_fine_ref,
    meso_ref, fine_ref, vec, old, cent, half_norm, perm, packed, got1, mid, got2,
    code1, code1_got, code2, last1, last1_got, last_mid, last2,
    ret1, ret1_got, ret_mid, back1, ret2,
    sums, counts, part, part_got, new_part, new_all,
    hot_ref, bin_hot, bin_ref, rank_ref, slot_ref, row_hot, inverse,
    load_sem, s1_send, s1_recv, s2_send, s2_recv, c1_send, c1_recv, c2_send, c2_recv,
    r1_send, r1_recv, r2_send, r2_recv, p_send, p_recv, n_send, n_recv, gate,
):
    x = lax.axis_index("dp")
    own = lax.axis_index("owner")
    y, z, c = lax.div(own, 16), lax.rem(lax.div(own, 2), 8), lax.rem(own, 2)

    def yz_peer(dy, dz):
        return (x, (lax.rem(y + dy, NY) * NZ + lax.rem(z + dz, NZ)) * NC + c)

    def xc_peer(j):
        return (lax.rem(x + lax.div(j, NC), NX), (y * NZ + z) * NC + lax.rem(c + lax.rem(j, NC), NC))

    def xc_back(j):
        return (lax.rem(x + NX - lax.div(j, NC), NX), (y * NZ + z) * NC + lax.rem(c + lax.rem(j, NC), NC))

    def yz_back(dy, dz):
        return yz_peer(NY - dy, NZ - dz)

    def near_z(way):
        odd = lax.rem(way, 2)
        return lax.rem(odd * lax.div(way + 1, 2) + (1 - odd) * lax.div(2 * NZ - way, 2), NZ)

    def start_of(q):
        return lax.div(SPLIT - q, SPLIT)

    def link(src, dst, send_sem, recv_sem, device):
        return pltpu.make_async_remote_copy(
            src_ref=src, dst_ref=dst, send_sem=send_sem, recv_sem=recv_sem,
            device_id=device, device_id_type=MESH,
        )

    here = (x, own)

    def arrived(dst, send_sem, recv_sem):
        link(dst, dst, send_sem, recv_sem, here).wait_recv()

    def left(src, send_sem, recv_sem):
        link(src, src, send_sem, recv_sem, here).wait_send()

    def block(way):
        return pl.ds(pl.multiple_of(way * BLOCK, BLOCK), BLOCK)

    def ways(at):
        return pl.ds(at * WAYS, WAYS)

    barrier = pltpu.get_barrier_semaphore()

    def greet(device):
        pl.semaphore_signal(barrier, 1, device_id=device, device_id_type=MESH)

    each(1, NZ, lambda dz: greet(yz_peer(0, dz)))
    each(1, NY, lambda dy: greet(yz_peer(dy, 0)))
    each(1, WAYS, lambda j: greet(xc_peer(j)))
    greeted = NZ + NY + WAYS - 3

    load_meso = pltpu.make_async_copy(meso_hbm, meso_ref, load_sem.at[3])
    load_fine = pltpu.make_async_copy(fine_hbm, fine_ref, load_sem.at[4])
    load_vec = pltpu.make_async_copy(vec_hbm, vec, load_sem.at[0])
    load_cent = pltpu.make_async_copy(cent_hbm, cent, load_sem.at[1])
    load_old = pltpu.make_async_copy(old_hbm, old, load_sem.at[2])
    for load in (load_meso, load_fine, load_vec, load_cent, load_old):
        load.start()

    load_meso.wait()
    load_fine.wait()
    meso = meso_ref[...].reshape(1, ROWS)
    fine = fine_ref[...].reshape(1, ROWS)
    to = meso >> 5
    dy = ((to >> 4) - y) & 3
    dz = (((to >> 1) & 7) - z) & 7
    way = ((((fine >> 4) - x) & 3) << 1) + ((to - c) & 1)
    z_near = jnp.where(dz <= 4, jnp.maximum(2 * dz - 1, 0), 2 * (NZ - dz))
    is_last = dy >= SPLIT
    hop1 = jnp.where(is_last, way, dz)
    hop2 = jnp.where(is_last, z_near, way)
    first = (dy << 3) + hop1
    bin_of = (first << 3) + hop2
    bin_ref[...] = bin_of

    def bin_rows(i):
        rows = pl.ds(pl.multiple_of(i * 64, 64), 64)
        bin_hot[rows, :] = (iota((64, ROWS), 0) + i * 64 == bin_of).astype(F32).astype(BF16)

    each(0, BINS // 64, bin_rows)

    def ranks(i):
        lanes = pl.ds(pl.multiple_of(i * LANES, LANES), LANES)
        before = (iota((ROWS, LANES), 0) < iota((ROWS, LANES), 1) + i * LANES).astype(F32).astype(BF16)
        ahead = dot(bin_hot[...], before)
        mine = iota((BINS, LANES), 0) == bin_ref[:, lanes]
        rank_ref[:, lanes] = jnp.sum(jnp.where(mine, ahead, 0.0), axis=0, keepdims=True).astype(I32)

    each(0, ROWS // LANES, ranks)
    rank = rank_ref[...]
    slot_ref[...] = bin_of * SLOTS + rank

    meso_code = ((meso & 31) + 1).astype(F32)
    fine_code = (fine & 15).astype(F32)

    def code_rows(hit, lane):
        hot = (iota((LANES, ROWS), 0) == lane).astype(F32).astype(BF16)
        high = jnp.where(hit, meso_code, 0.0).astype(BF16)
        low = jnp.where(hit, fine_code, 0.0).astype(BF16)
        return 16.0 * dot(high, hot, NT) + dot(low, hot, NT)

    codes = code_rows(iota((EARLY, ROWS), 0) == first, hop2 * SLOTS + rank)
    for r in range(EARLY):
        code1[r] = codes[r : r + 1, :]
    load_vec.wait()

    def pack(q):
        def hot_rows(i):
            rows = pl.ds(pl.multiple_of(i * 64, 64), 64)
            at = iota((64, ROWS), 0) + (q * CHUNK_ROWS + i * 64)
            hot_ref[rows, :] = (at == slot_ref[...]).astype(F32).astype(BF16)

        def columns(i):
            lanes = pl.ds(pl.multiple_of(i * 256, 256), 256)
            packed[q, :, lanes] = dot(hot_ref[...], vec[:, lanes]).astype(BF16)

        each(0, CHUNK_ROWS // 64, hot_rows)
        each(0, D // 256, columns)

    def leave_late(q):
        late = q - SPLIT

        def code(way):
            at = ways(late * WAYS + way)
            link(last1.at[at], last1_got.at[at], c1_send.at[q], c1_recv.at[q], xc_peer(way)).start()

        def rows(way):
            link(packed.at[q, block(way)], got1.at[q, block(way)], s1_send.at[q], s1_recv.at[q], xc_peer(way)).start()

        pack(q)
        last1_got[ways(late * WAYS)] = last1[ways(late * WAYS)]
        got1[q, 0:BLOCK, :] = packed[q, 0:BLOCK, :]
        each(1, WAYS, code)
        each(1, WAYS, rows)

    def leave_early(q):
        def code(way):
            at = q * WAYS + way
            link(code1.at[at], code1_got.at[at], c1_send.at[q], c1_recv.at[q], yz_peer(q, way)).start()

        def rows(way):
            link(packed.at[q, block(way)], got1.at[q, block(way)], s1_send.at[q], s1_recv.at[q], yz_peer(q, way)).start()

        each(start_of(q), WAYS, code)
        each(start_of(q), WAYS, rows)

    def signal(dy):
        pl.semaphore_signal(gate, 1, device_id=yz_peer(dy, 0), device_id_type=MESH)

    pack(0)
    code1_got[0] = code1[0]
    got1[0, 0:BLOCK, :] = packed[0, 0:BLOCK, :]
    pl.semaphore_wait(barrier, greeted)
    leave_early(0)
    each(1, NY, signal)
    codes = code_rows(iota((LATE * PAIRS, ROWS), 0) + SPLIT * PAIRS == bin_of, hop1 * SLOTS + rank)
    for r in range(LATE * PAIRS):
        last1[r] = codes[r : r + 1, :]
    each(SPLIT, CHUNKS, leave_late)
    each(1, SPLIT, pack)
    pl.semaphore_wait(gate, NY - 1)
    each(1, SPLIT, leave_early)

    def perm_rows(i):
        rows = pl.ds(pl.multiple_of(i * 64, 64), 64)
        out_row = iota((64, CHUNK_ROWS), 0) + i * 64
        in_row = iota((64, CHUNK_ROWS), 1)
        out_pair, in_pair = div6(out_row), div6(in_row)
        swapped = ((out_pair & 7) << 3) + (out_pair >> 3)
        hit = in_row - 6 * in_pair + 6 * swapped == out_row - 6 * out_pair + 6 * in_pair
        perm[rows, :] = hit.astype(F32).astype(BF16)

    each(0, CHUNK_ROWS // 64, perm_rows)

    def regroup(q):
        def columns(i):
            lanes = pl.ds(pl.multiple_of(i * 256, 256), 256)
            mid[q, :, lanes] = dot(perm[...], got1[q, :, lanes]).astype(BF16)

        each(0, D // 256, columns)

    def pass_late(q):
        late = q - SPLIT

        def codes_on(way):
            at = late * WAYS + way
            link(last_mid.at[at], last2.at[at], c2_send.at[q], c2_recv.at[q], yz_peer(q, near_z(way))).start()

        def rows_on(way):
            half = s2_recv.at[SPLIT + late * 2 + lax.div(way, WAYS // 2)]
            link(mid.at[q, block(way)], got2.at[q, block(way)], s2_send.at[q], half, yz_peer(q, near_z(way))).start()

        arrived(last1_got.at[pl.ds(late * PAIRS + WAYS, PAIRS - WAYS)], c1_send.at[q], c1_recv.at[q])
        last_mid[ways(late)] = sum(last1_got[pl.ds(late * PAIRS + way * WAYS, WAYS)] for way in range(WAYS))
        each(0, WAYS, codes_on)
        arrived(got1.at[q, pl.ds(BLOCK, CHUNK_ROWS - BLOCK)], s1_send.at[q], s1_recv.at[q])
        regroup(q)
        each(0, WAYS, rows_on)

    each(SPLIT, CHUNKS, pass_late)

    load_cent.wait()

    def norms(i):
        rows = pl.ds(pl.multiple_of(i * 32, 32), 32)
        wide = cent[rows, :].astype(F32)
        half_norm[rows, :] = 0.5 * jnp.sum(wide * wide, axis=1, keepdims=True)

    each(0, MESO_DEV * KF // 32, norms)

    load_old.wait()

    def begin(m):
        rows = pl.ds(pl.multiple_of(m * FGROUP, FGROUP), FGROUP)
        mine = pl.ds(pl.multiple_of(m * KF + x * FGROUP, FGROUP), FGROUP)
        sums[rows, :] = cent[mine, :].astype(F32) - old[pl.ds(m, 1), :]

    each(0, MESO_DEV, begin)
    from_row = jnp.where(is_last, bin_of - SPLIT * PAIRS + EARLY, first)

    def from_rows(i):
        rows = pl.ds(pl.multiple_of(i * 16, 16), 16)
        row_hot[rows, :] = (iota((16, ROWS), 0) + i * 16 == from_row).astype(F32).astype(BF16)

    each(0, (EARLY + LATE * PAIRS) // 16, from_rows)
    counts[...] = jnp.zeros_like(counts)
    part[...] = jnp.zeros_like(part)

    def codes_from(tile, hit, pick):
        tile = tile.astype(I32)
        high = dot((tile >> 4).astype(F32).astype(BF16), pick)
        low = dot((tile & 15).astype(F32).astype(BF16), pick)
        high = jnp.sum(jnp.where(hit, high, 0.0), axis=0, keepdims=True)
        low = jnp.sum(jnp.where(hit, low, 0.0), axis=0, keepdims=True)
        return (high.astype(I32) - 1, low.astype(I32))

    def add_meso(members, high):
        hot = (iota((MESO_DEV, members.shape[0]), 0) == high).astype(F32)
        part[:, 0:D] += dot(hot.astype(BF16), members)
        part[:, D : D + LANES] += jnp.broadcast_to(jnp.sum(hot, axis=1, keepdims=True), (MESO_DEV, LANES))

    def nearest(members, high):
        size = members.shape[0]
        step = LANES if size % LANES == 0 else size
        eye = iota((step, step), 0) == iota((step, step), 1)
        norm = jnp.concatenate(
            [
                jnp.sum(
                    jnp.where(eye, dot(members[t : t + step], members[t : t + step], NT), 0.0), axis=0, keepdims=True
                )
                for t in range(0, size, step)
            ],
            axis=1,
        )

        best = jnp.zeros((1, size), F32)
        for i in range(0, MESO_DEV * KF, 1024):
            cross = dot(cent[i : i + 1024, :], members, NT) - half_norm[i : i + 1024, :]
            for t in range(0, 1024, KF):
                top = jnp.max(cross[t : t + KF], axis=0, keepdims=True)
                best = jnp.where(high == (i + t) // KF, top, best)
        return jnp.where(high >= 0, (norm - 2.0 * best) * (1.0 / D), 0.0)

    def add_fine(members, high, low):
        code = (high << 4) + low
        size = members.shape[0]

        def step(i):
            rows = pl.ds(pl.multiple_of(i * 128, 128), 128)
            hot = (iota((128, size), 0) + i * 128 == code).astype(F32)
            sums[rows, :] += dot(hot.astype(BF16), members)
            counts[rows, :] += jnp.sum(hot, axis=1, keepdims=True)

        each(0, MESO_DEV * FGROUP // 128, step)

    def spread_of(near, hit, pick):
        return sum(dot(piece, pick, NT) for piece in split3(jnp.where(hit, near, 0.0)))

    def early_rows(step, q, ref, send_sem, recv_sem):
        @pl.when(q == 0)
        def _():
            step(ref(1), send_sem, recv_sem)

        @pl.when(q > 0)
        def _():
            step(ref(0), send_sem, recv_sem)

    def tail_of(ref, q):
        return lambda way: ref.at[pl.ds(q * WAYS + way, WAYS - way)]

    def rows_of(ref, q):
        return lambda way: ref.at[q, pl.ds(way * BLOCK, CHUNK_ROWS - way * BLOCK)]

    def tiles_of(ref, q):
        return ref.at[pl.ds(q * PAIRS + WAYS, PAIRS - WAYS)]

    def pass_on(q):
        def codes_on(way):
            at = q * WAYS + way
            link(code1_got.at[ways(q)], code2.at[ways(at)], c2_send.at[q], c2_recv.at[q], xc_peer(way)).start()

        def rows_on(way):
            link(mid.at[q, block(way)], got2.at[q, block(way)], s2_send.at[q], s2_recv.at[q], xc_peer(way)).start()

        early_rows(arrived, q, tail_of(code1_got, q), c1_send.at[q], c1_recv.at[q])
        code2[ways(q * WAYS)] = code1_got[ways(q)]
        each(1, WAYS, codes_on)
        early_rows(arrived, q, rows_of(got1, q), s1_send.at[q], s1_recv.at[q])
        regroup(q)
        got2[q, 0:BLOCK, :] = mid[q, 0:BLOCK, :]
        each(1, WAYS, rows_on)

    def work(q):
        row = iota((LANES, CHUNK_ROWS), 1)
        pick = (iota((LANES, CHUNK_ROWS), 0) == div48(row) * SLOTS + row - 6 * div6(row)).astype(F32).astype(BF16)
        hit = iota((WAYS * WAYS, CHUNK_ROWS), 0) == div6(iota((WAYS * WAYS, CHUNK_ROWS), 1))
        arrived(tiles_of(code2, q), c2_send.at[q], c2_recv.at[q])
        tile = code2[pl.ds(q * PAIRS, PAIRS)].reshape(PAIRS, LANES)
        high, low = codes_from(tile, hit, pick)
        arrived(got2.at[q, pl.ds(BLOCK, CHUNK_ROWS - BLOCK)], s2_send.at[q], s2_recv.at[q])
        members = got2[q]
        spread = spread_of(nearest(members, high), hit, pick)
        for r in range(PAIRS):
            ret1[q * PAIRS + r] = spread[r : r + 1, :]
        ret1_got[ways(q * WAYS)] = ret1[ways(q * WAYS)]

        def back(way):
            at = ways(q * WAYS + way)
            link(ret1.at[at], ret1_got.at[at], r1_send.at[q], r1_recv.at[q], xc_back(way)).start()

        each(1, WAYS, back)
        add_meso(members, high)
        add_fine(members, high, low)

    def pass_back(q):
        def back(way):
            at = q * WAYS + way
            link(ret_mid.at[at], ret2.at[at], r2_send.at[q], r2_recv.at[q], yz_back(q, way)).start()

        arrived(tiles_of(ret1_got, q), r1_send.at[q], r1_recv.at[q])
        ret_mid[ways(q)] = sum(ret1_got[pl.ds((q * WAYS + way) * WAYS, WAYS)] for way in range(WAYS))
        each(start_of(q), WAYS, back)

    def turn(i):
        pass_on(i)

        @pl.when(i > 0)
        def _():
            pass_back(i - 1)

        work(i)

    each(0, SPLIT, turn)

    def early_left(q):
        early_rows(left, q, rows_of(packed, q), s1_send.at[q], s1_recv.at[q])
        early_rows(left, q, tail_of(code1, q), c1_send.at[q], c1_recv.at[q])
        left(mid.at[q, pl.ds(BLOCK, CHUNK_ROWS - BLOCK)], s2_send.at[q], s2_recv.at[q])
        left(tiles_of(code2, q), c2_send.at[q], c2_recv.at[q])
        left(tiles_of(ret1, q), r1_send.at[q], r1_recv.at[q])

    def late_left(q):
        left(packed.at[q, pl.ds(BLOCK, CHUNK_ROWS - BLOCK)], s1_send.at[q], s1_recv.at[q])
        left(tiles_of(last1, q - SPLIT), c1_send.at[q], c1_recv.at[q])

    back_x = [lax.rem(x + NX - dx, NX) for dx in range(NX)]
    back_c = [lax.rem(c + dc, NC) for dc in range(NC)]

    def late_half(n):
        q = SPLIT + lax.div(n, 2)
        h = lax.rem(n, 2)
        late = lax.div(n, 2)
        row = iota((LANES, HALF), 1) + h * HALF
        pick = (iota((LANES, HALF), 0) == row - 48 * div48(row)).astype(F32).astype(BF16)
        hit = iota((WAYS, HALF), 0) == div48(iota((WAYS, HALF), 1) + h * HALF)

        @pl.when(h == 0)
        def _():
            arrived(last2.at[ways(late)], c2_send.at[q], c2_recv.at[q])

        high, low = codes_from(last2[ways(late)].reshape(WAYS, LANES), hit, pick)

        half = pl.ds(pl.multiple_of(h * HALF, HALF), HALF)
        arrived(got2.at[q, half], s2_send.at[q], s2_recv.at[SPLIT + n])
        members = got2[q, half, :]
        add_meso(members, high)

        @pl.when(n == 2 * LATE - 1)
        def _():
            def share_out(dx):
                share = pl.ds(pl.multiple_of(lax.rem(x + dx, NX) * SHARE, SHARE), SHARE)
                device = xc_peer(dx * NC)
                link(part.at[share], part_got.at[dx - 1], p_send, p_recv, device).start()

            each(1, NX, share_out)

        own_hit = iota((WAYS, HALF), 0) == div48(iota((WAYS, HALF), 1))
        spread = spread_of(nearest(members, high), own_hit, pick)
        for r in range(WAYS // 2):
            back1[late * WAYS + h * (WAYS // 2) + r] = spread[r : r + 1, :]

        def back(i):
            way = h * (WAYS // 2) + i
            row = late * WAYS + way
            to_row = EARLY + late * PAIRS + way
            to_yz = (lax.rem(y + NY - q, NY) * NZ + lax.rem(z + NZ - near_z(way), NZ)) * NC
            for j in range(WAYS):
                device = (back_x[j // NC], to_yz + back_c[j % NC])
                link(back1.at[row], ret2.at[to_row + j * WAYS], r2_send.at[q], r2_recv.at[q], device).start()

        each(0, WAYS // 2, back)
        add_fine(members, high, low)

        @pl.when(n == 1)
        def _():
            pass_back(SPLIT - 1)
            each(0, SPLIT, early_left)
            each(SPLIT, CHUNKS, late_left)

    each(0, 2 * LATE, late_half)
    ret2[0] = ret_mid[0]

    inverse[...] = 1.0 / (counts[...] + 1.0)

    arrived(part_got, p_send, p_recv)
    share = pl.ds(pl.multiple_of(x * SHARE, SHARE), SHARE)
    total = (part[share, :] + part_got[1]) + (part_got[0] + part_got[2])
    new_part[...] = (total[:, 0:D] + old[share, :]) / (total[:, D : D + 1] + 1.0)

    def hand_out(dx):
        link(new_part, new_all.at[dx - 1], n_send, n_recv, xc_peer(dx * NC)).start()

    each(1, NX, hand_out)
    new_meso_ref[share, :] = new_part[...]

    def finish(block):
        first_meso = block * SHARE
        for m in range(SHARE):
            rows = pl.ds(pl.multiple_of((first_meso + m) * FGROUP, FGROUP), FGROUP)
            new_fine_ref[rows, :] = (sums[rows, :] + new_meso_ref[pl.ds(first_meso + m, 1), :]) * inverse[rows, :]

    finish(x)

    mine = iota((LANES, ROWS), 0) == jnp.where(is_last, hop1, hop2) * SLOTS + rank
    arrived(ret2.at[pl.ds(1, WAYS - 1)], r2_send.at[0], r2_recv.at[0])
    for q in range(1, SPLIT):
        arrived(ret2.at[ways(q)], r2_send.at[q], r2_recv.at[q])
    for q in range(SPLIT, CHUNKS):
        arrived(ret2.at[pl.ds(EARLY + (q - SPLIT) * PAIRS, PAIRS)], r2_send.at[q], r2_recv.at[q])
    returned = ret2[...].reshape(EARLY + LATE * PAIRS, LANES)
    picked = sum(dot(piece, row_hot[...], TN) for piece in split3(returned))
    near_ref[...] = jnp.sum(jnp.where(mine, picked, 0.0), axis=0, keepdims=True).reshape(ROWS)

    arrived(new_all, n_send, n_recv)

    def finish_other(dx):
        block = lax.rem(x + NX - dx, NX)
        new_meso_ref[pl.ds(pl.multiple_of(block * SHARE, SHARE), SHARE), :] = new_all[dx - 1]
        finish(block)

    each(1, NX, finish_other)

    left(code1.at[pl.ds(1, WAYS - 1)], r2_send.at[0], r2_recv.at[0])
    for q in range(1, SPLIT):
        left(code1.at[ways(q)], r2_send.at[q], r2_recv.at[q])
    for q in range(SPLIT, CHUNKS):
        left(mid.at[q], s2_send.at[q], s2_recv.at[q])
        left(last_mid.at[ways(q - SPLIT)], c2_send.at[q], c2_recv.at[q])
        left(last1.at[pl.ds((q - SPLIT) * PAIRS, PAIRS)], r2_send.at[q], r2_recv.at[q])
    left(part_got, p_send, p_recv)
    left(new_all, n_send, n_recv)


def body(vectors, meso_labels, fine_labels, meso_centroids, fine_centroids):
    hbm = pl.BlockSpec(memory_space=pl.ANY)
    vmem = pl.BlockSpec(memory_space=pltpu.VMEM)
    dma = pltpu.SemaphoreType.DMA
    outs = (((ROWS,), F32), ((MESO_DEV, D), F32), ((MESO_DEV * FGROUP, D), F32))

    def row(count):
        return pltpu.VMEM((count, 1, LANES), F32)

    near, new_meso, new_fine = pl.pallas_call(
        kernel,
        out_shape=tuple(pltpu.VMEM(*out) for out in outs),
        in_specs=[hbm] * 5,
        out_specs=(vmem,) * 3,
        scratch_shapes=[
            pltpu.VMEM((ROWS,), I32),
            pltpu.VMEM((ROWS,), I32),
            pltpu.VMEM((ROWS, D), BF16),
            pltpu.VMEM((MESO_DEV, D), F32),
            pltpu.VMEM((MESO_DEV * KF, D), BF16),
            pltpu.VMEM((MESO_DEV * KF, 1), F32),
            pltpu.VMEM((CHUNK_ROWS, CHUNK_ROWS), BF16),
            pltpu.VMEM((CHUNKS, CHUNK_ROWS, D), BF16),
            pltpu.VMEM((CHUNKS, CHUNK_ROWS, D), BF16),
            pltpu.VMEM((CHUNKS, CHUNK_ROWS, D), BF16),
            pltpu.VMEM((CHUNKS, CHUNK_ROWS, D), BF16),
            row(EARLY), row(EARLY), row(EARLY * WAYS),
            row(LATE * PAIRS), row(LATE * PAIRS), row(LATER), row(LATER),
            row(EARLY * WAYS), row(EARLY * WAYS), row(EARLY),
            row(LATER), row(EARLY + LATE * PAIRS),
            pltpu.VMEM((MESO_DEV * FGROUP, D), F32),
            pltpu.VMEM((MESO_DEV * FGROUP, 1), F32),
            pltpu.VMEM((MESO_DEV, D + LANES), F32),
            pltpu.VMEM((NX - 1, SHARE, D + LANES), F32),
            pltpu.VMEM((SHARE, D), F32),
            pltpu.VMEM((NX - 1, SHARE, D), F32),
            pltpu.VMEM((CHUNK_ROWS, ROWS), BF16),
            pltpu.VMEM((BINS, ROWS), BF16),
            pltpu.VMEM((1, ROWS), I32),
            pltpu.VMEM((1, ROWS), I32),
            pltpu.VMEM((1, ROWS), I32),
            pltpu.VMEM((EARLY + LATE * PAIRS, ROWS), BF16),
            pltpu.VMEM((MESO_DEV * FGROUP, 1), F32),
            dma((5,)),
        ]
        + [dma((CHUNKS,)), dma((CHUNKS,)), dma((CHUNKS,)), dma((SPLIT + 2 * LATE,))]
        + [dma((CHUNKS,)) for _ in range(8)]
        + [dma] * 4
        + [pltpu.SemaphoreType.REGULAR],
        compiler_params=pltpu.CompilerParams(
            collective_id=0, has_side_effects=True, vmem_limit_bytes=61 * 2**20
        ),
    )(
        meso_labels,
        fine_labels,
        vectors,
        meso_centroids,
        fine_centroids.reshape(MESO_DEV * KF, D),
    )
    return (near, new_meso, new_fine.reshape(MESO_DEV, FGROUP, D))


def solution(mesh):
    return jax.shard_map(
        body,
        mesh=mesh,
        in_specs=(
            P(("dp", "owner"), None),
            P(("dp", "owner")),
            P(("dp", "owner")),
            P("owner", None),
            P("owner", None, None),
        ),
        out_specs=(P(("dp", "owner")), P("owner", None), P("owner", "dp", None)),
        check_vma=False,
    )
```

```python
import jax
import jax.numpy as jnp
from jax import lax
from jax.experimental import pallas as pl
from jax.experimental.pallas import tpu as pltpu
from jax.sharding import PartitionSpec as P

MESH = pl.DeviceIdType.MESH
D = 1024
ROWS = 768
KF = 64
MESO_DEV = 32
FGROUP = 16
SLOTS = 6
NX, NY, NZ, NC = 4, 4, 8, 2
CHUNKS = NY
WAYS = 8
BLOCK = WAYS * SLOTS
CHUNK_ROWS = WAYS * BLOCK
BINS = CHUNKS * WAYS * WAYS
LANES = 128
SHARE = MESO_DEV // NX
SPLIT = 2
LATE = CHUNKS - SPLIT
EARLY = SPLIT * WAYS
LATER = LATE * WAYS
PAIRS = WAYS * WAYS
HALF = CHUNK_ROWS // 2

F32, BF16, I32 = jnp.float32, jnp.bfloat16, jnp.int32
NT = (((1,), (1,)), ((), ()))
TN = (((0,), (0,)), ((), ()))


def iota(shape, dim):
    return lax.broadcasted_iota(I32, shape, dim)


def div6(v):
    return (v * 10923) >> 16


def div48(v):
    return div6(v >> 3)


def split3(v):
    first = v.astype(BF16)
    rest = v - first.astype(F32)
    second = rest.astype(BF16)
    third = (rest - second.astype(F32)).astype(BF16)
    return (first, second, third)


def dot(a, b, dims=(((1,), (0,)), ((), ()))):
    return lax.dot_general(a, b, dims, preferred_element_type=F32)


def each(low, high, step):
    def body(i, carry):
        step(i)
        return carry

    lax.fori_loop(low, high, body, 0)


def kernel(
    meso_hbm, fine_hbm, vec_hbm, old_hbm, cent_hbm,
    near_ref, new_meso_ref, new_fine_ref,
    meso_ref, fine_ref, vec, old, cent, half_norm, perm, packed, got1, mid, got2,
    code1, code1_got, code2, last1, last1_got, last_mid, last2,
    ret1, ret1_got, ret_mid, back1, ret2,
    sums, counts, part, part_got, new_part, new_all,
    hot_ref, bin_hot, bin_ref, rank_ref, slot_ref, row_hot, inverse,
    load_sem, s1_send, s1_recv, s2_send, s2_recv, c1_send, c1_recv, c2_send, c2_recv,
    r1_send, r1_recv, r2_send, r2_recv, p_send, p_recv, n_send, n_recv, gate,
):
    x = lax.axis_index("dp")
    own = lax.axis_index("owner")
    y, z, c = lax.div(own, 16), lax.rem(lax.div(own, 2), 8), lax.rem(own, 2)

    def yz_peer(dy, dz):
        return (x, (lax.rem(y + dy, NY) * NZ + lax.rem(z + dz, NZ)) * NC + c)

    def xc_peer(j):
        return (lax.rem(x + lax.div(j, NC), NX), (y * NZ + z) * NC + lax.rem(c + lax.rem(j, NC), NC))

    def xc_back(j):
        return (lax.rem(x + NX - lax.div(j, NC), NX), (y * NZ + z) * NC + lax.rem(c + lax.rem(j, NC), NC))

    def yz_back(dy, dz):
        return yz_peer(NY - dy, NZ - dz)

    def near_z(way):
        odd = lax.rem(way, 2)
        return lax.rem(odd * lax.div(way + 1, 2) + (1 - odd) * lax.div(2 * NZ - way, 2), NZ)

    def start_of(q):
        return lax.div(SPLIT - q, SPLIT)

    def link(src, dst, send_sem, recv_sem, device):
        return pltpu.make_async_remote_copy(
            src_ref=src, dst_ref=dst, send_sem=send_sem, recv_sem=recv_sem,
            device_id=device, device_id_type=MESH,
        )

    here = (x, own)

    def arrived(dst, send_sem, recv_sem):
        link(dst, dst, send_sem, recv_sem, here).wait_recv()

    def left(src, send_sem, recv_sem):
        link(src, src, send_sem, recv_sem, here).wait_send()

    def block(way):
        return pl.ds(pl.multiple_of(way * BLOCK, BLOCK), BLOCK)

    def ways(at):
        return pl.ds(at * WAYS, WAYS)

    barrier = pltpu.get_barrier_semaphore()

    def greet(device):
        pl.semaphore_signal(barrier, 1, device_id=device, device_id_type=MESH)

    for dz in (4, 3, 5, 2, 6, 1, 7):
        greet(yz_peer(0, dz))
    for dy in (2, 1, 3):
        greet(yz_peer(dy, 0))
    for j in range(WAYS - 1, 0, -1):
        greet((lax.rem(x + j // NC, NX), (y * NZ + z) * NC + lax.rem(c + j % NC, NC)))
    greeted = NZ + NY + WAYS - 3

    load_meso = pltpu.make_async_copy(meso_hbm, meso_ref, load_sem.at[3])
    load_fine = pltpu.make_async_copy(fine_hbm, fine_ref, load_sem.at[4])
    load_vec = pltpu.make_async_copy(vec_hbm, vec, load_sem.at[0])
    load_cent = pltpu.make_async_copy(cent_hbm, cent, load_sem.at[1])
    load_old = pltpu.make_async_copy(old_hbm, old, load_sem.at[2])
    for load in (load_meso, load_fine, load_vec, load_cent, load_old):
        load.start()

    load_meso.wait()
    load_fine.wait()
    meso = meso_ref[...].reshape(1, ROWS)
    fine = fine_ref[...].reshape(1, ROWS)
    to = meso >> 5
    dy = ((to >> 4) - y) & 3
    dz = (((to >> 1) & 7) - z) & 7
    way = ((((fine >> 4) - x) & 3) << 1) + ((to - c) & 1)
    z_near = jnp.where(dz <= 4, jnp.maximum(2 * dz - 1, 0), 2 * (NZ - dz))
    is_last = dy >= SPLIT
    hop1 = jnp.where(is_last, way, dz)
    hop2 = jnp.where(is_last, z_near, way)
    first = (dy << 3) + hop1
    bin_of = (first << 3) + hop2
    bin_ref[...] = bin_of

    def bin_rows(i):
        rows = pl.ds(pl.multiple_of(i * 64, 64), 64)
        bin_hot[rows, :] = (iota((64, ROWS), 0) + i * 64 == bin_of).astype(F32).astype(BF16)

    each(0, BINS // 64, bin_rows)

    def ranks(i):
        lanes = pl.ds(pl.multiple_of(i * LANES, LANES), LANES)
        before = (iota((ROWS, LANES), 0) < iota((ROWS, LANES), 1) + i * LANES).astype(F32).astype(BF16)
        ahead = dot(bin_hot[...], before)
        mine = iota((BINS, LANES), 0) == bin_ref[:, lanes]
        rank_ref[:, lanes] = jnp.sum(jnp.where(mine, ahead, 0.0), axis=0, keepdims=True).astype(I32)

    each(0, ROWS // LANES, ranks)
    rank = rank_ref[...]
    slot_ref[...] = bin_of * SLOTS + rank

    meso_code = ((meso & 31) + 1).astype(F32)
    fine_code = (fine & 15).astype(F32)

    def code_rows(hit, lane):
        hot = (iota((LANES, ROWS), 0) == lane).astype(F32).astype(BF16)
        high = jnp.where(hit, meso_code, 0.0).astype(BF16)
        low = jnp.where(hit, fine_code, 0.0).astype(BF16)
        return 16.0 * dot(high, hot, NT) + dot(low, hot, NT)

    codes = code_rows(iota((EARLY, ROWS), 0) == first, hop2 * SLOTS + rank)
    for r in range(EARLY):
        code1[r] = codes[r : r + 1, :]
    load_vec.wait()

    def pack(q):
        def hot_rows(i):
            rows = pl.ds(pl.multiple_of(i * 64, 64), 64)
            at = iota((64, ROWS), 0) + (q * CHUNK_ROWS + i * 64)
            hot_ref[rows, :] = (at == slot_ref[...]).astype(F32).astype(BF16)

        def columns(i):
            lanes = pl.ds(pl.multiple_of(i * 256, 256), 256)
            packed[q, :, lanes] = dot(hot_ref[...], vec[:, lanes]).astype(BF16)

        each(0, CHUNK_ROWS // 64, hot_rows)
        each(0, D // 256, columns)

    def leave_late(q):
        late = q - SPLIT

        def code(way):
            at = ways(late * WAYS + way)
            link(last1.at[at], last1_got.at[at], c1_send.at[q], c1_recv.at[q], xc_peer(way)).start()

        def rows(way):
            link(packed.at[q, block(way)], got1.at[q, block(way)], s1_send.at[q], s1_recv.at[q], xc_peer(way)).start()

        pack(q)
        last1_got[ways(late * WAYS)] = last1[ways(late * WAYS)]
        got1[q, 0:BLOCK, :] = packed[q, 0:BLOCK, :]
        each(1, WAYS, code)
        each(1, WAYS, rows)

    def leave_early(q):
        def code(i):
            way = near_z(i)
            at = q * WAYS + way
            link(code1.at[at], code1_got.at[at], c1_send.at[q], c1_recv.at[q], yz_peer(q, way)).start()

        def rows(i):
            way = near_z(i)
            link(packed.at[q, block(way)], got1.at[q, block(way)], s1_send.at[q], s1_recv.at[q], yz_peer(q, way)).start()

        each(start_of(q), WAYS, code)
        each(start_of(q), WAYS, rows)

    def signal(dy):
        pl.semaphore_signal(gate, 1, device_id=yz_peer(dy, 0), device_id_type=MESH)

    pack(0)
    code1_got[0] = code1[0]
    got1[0, 0:BLOCK, :] = packed[0, 0:BLOCK, :]
    pl.semaphore_wait(barrier, greeted)
    leave_early(0)
    each(1, NY, signal)
    codes = code_rows(iota((LATE * PAIRS, ROWS), 0) + SPLIT * PAIRS == bin_of, hop1 * SLOTS + rank)
    for r in range(LATE * PAIRS):
        last1[r] = codes[r : r + 1, :]
    each(SPLIT, CHUNKS, leave_late)
    each(1, SPLIT, pack)
    pl.semaphore_wait(gate, NY - 1)
    each(1, SPLIT, leave_early)

    def perm_rows(i):
        rows = pl.ds(pl.multiple_of(i * 64, 64), 64)
        out_row = iota((64, CHUNK_ROWS), 0) + i * 64
        in_row = iota((64, CHUNK_ROWS), 1)
        out_pair, in_pair = div6(out_row), div6(in_row)
        swapped = ((out_pair & 7) << 3) + (out_pair >> 3)
        hit = in_row - 6 * in_pair + 6 * swapped == out_row - 6 * out_pair + 6 * in_pair
        perm[rows, :] = hit.astype(F32).astype(BF16)

    each(0, CHUNK_ROWS // 64, perm_rows)

    def regroup(q):
        def columns(i):
            lanes = pl.ds(pl.multiple_of(i * 256, 256), 256)
            mid[q, :, lanes] = dot(perm[...], got1[q, :, lanes]).astype(BF16)

        each(0, D // 256, columns)

    def pass_late(q):
        late = q - SPLIT

        def codes_on(way):
            at = late * WAYS + way
            link(last_mid.at[at], last2.at[at], c2_send.at[q], c2_recv.at[q], yz_peer(q, near_z(way))).start()

        def rows_on(way):
            half = s2_recv.at[SPLIT + late * 2 + lax.div(way, WAYS // 2)]
            link(mid.at[q, block(way)], got2.at[q, block(way)], s2_send.at[q], half, yz_peer(q, near_z(way))).start()

        arrived(last1_got.at[pl.ds(late * PAIRS + WAYS, PAIRS - WAYS)], c1_send.at[q], c1_recv.at[q])
        last_mid[ways(late)] = sum(last1_got[pl.ds(late * PAIRS + way * WAYS, WAYS)] for way in range(WAYS))
        each(0, WAYS, codes_on)
        arrived(got1.at[q, pl.ds(BLOCK, CHUNK_ROWS - BLOCK)], s1_send.at[q], s1_recv.at[q])
        regroup(q)
        each(0, WAYS, rows_on)

    each(SPLIT, CHUNKS, pass_late)

    load_cent.wait()

    def norms(i):
        rows = pl.ds(pl.multiple_of(i * 32, 32), 32)
        wide = cent[rows, :].astype(F32)
        half_norm[rows, :] = 0.5 * jnp.sum(wide * wide, axis=1, keepdims=True)

    each(0, MESO_DEV * KF // 32, norms)

    load_old.wait()

    def begin(m):
        rows = pl.ds(pl.multiple_of(m * FGROUP, FGROUP), FGROUP)
        mine = pl.ds(pl.multiple_of(m * KF + x * FGROUP, FGROUP), FGROUP)
        sums[rows, :] = cent[mine, :].astype(F32) - old[pl.ds(m, 1), :]

    each(0, MESO_DEV, begin)
    from_row = jnp.where(is_last, bin_of - SPLIT * PAIRS + EARLY, first)

    def from_rows(i):
        rows = pl.ds(pl.multiple_of(i * 16, 16), 16)
        row_hot[rows, :] = (iota((16, ROWS), 0) + i * 16 == from_row).astype(F32).astype(BF16)

    each(0, (EARLY + LATE * PAIRS) // 16, from_rows)
    counts[...] = jnp.zeros_like(counts)
    part[...] = jnp.zeros_like(part)

    def codes_from(tile, hit, pick):
        tile = tile.astype(I32)
        high = dot((tile >> 4).astype(F32).astype(BF16), pick)
        low = dot((tile & 15).astype(F32).astype(BF16), pick)
        high = jnp.sum(jnp.where(hit, high, 0.0), axis=0, keepdims=True)
        low = jnp.sum(jnp.where(hit, low, 0.0), axis=0, keepdims=True)
        return (high.astype(I32) - 1, low.astype(I32))

    def add_meso(members, high):
        hot = (iota((MESO_DEV, members.shape[0]), 0) == high).astype(F32)
        part[:, 0:D] += dot(hot.astype(BF16), members)
        part[:, D : D + LANES] += jnp.broadcast_to(jnp.sum(hot, axis=1, keepdims=True), (MESO_DEV, LANES))

    def nearest(members, high):
        size = members.shape[0]
        step = LANES if size % LANES == 0 else size
        eye = iota((step, step), 0) == iota((step, step), 1)
        norm = jnp.concatenate(
            [
                jnp.sum(
                    jnp.where(eye, dot(members[t : t + step], members[t : t + step], NT), 0.0), axis=0, keepdims=True
                )
                for t in range(0, size, step)
            ],
            axis=1,
        )

        best = jnp.zeros((1, size), F32)
        for i in range(0, MESO_DEV * KF, 1024):
            cross = dot(cent[i : i + 1024, :], members, NT) - half_norm[i : i + 1024, :]
            for t in range(0, 1024, KF):
                top = jnp.max(cross[t : t + KF], axis=0, keepdims=True)
                best = jnp.where(high == (i + t) // KF, top, best)
        return jnp.where(high >= 0, (norm - 2.0 * best) * (1.0 / D), 0.0)

    def add_fine(members, high, low):
        code = (high << 4) + low
        size = members.shape[0]

        def step(i):
            rows = pl.ds(pl.multiple_of(i * 128, 128), 128)
            hot = (iota((128, size), 0) + i * 128 == code).astype(F32)
            sums[rows, :] += dot(hot.astype(BF16), members)
            counts[rows, :] += jnp.sum(hot, axis=1, keepdims=True)

        each(0, MESO_DEV * FGROUP // 128, step)

    def spread_of(near, hit, pick):
        return sum(dot(piece, pick, NT) for piece in split3(jnp.where(hit, near, 0.0)))

    def early_rows(step, q, ref, send_sem, recv_sem):
        @pl.when(q == 0)
        def _():
            step(ref(1), send_sem, recv_sem)

        @pl.when(q > 0)
        def _():
            step(ref(0), send_sem, recv_sem)

    def tail_of(ref, q):
        return lambda way: ref.at[pl.ds(q * WAYS + way, WAYS - way)]

    def rows_of(ref, q):
        return lambda way: ref.at[q, pl.ds(way * BLOCK, CHUNK_ROWS - way * BLOCK)]

    def tiles_of(ref, q):
        return ref.at[pl.ds(q * PAIRS + WAYS, PAIRS - WAYS)]

    def pass_on(q):
        def codes_on(way):
            at = q * WAYS + way
            link(code1_got.at[ways(q)], code2.at[ways(at)], c2_send.at[q], c2_recv.at[q], xc_peer(way)).start()

        def rows_on(way):
            link(mid.at[q, block(way)], got2.at[q, block(way)], s2_send.at[q], s2_recv.at[q], xc_peer(way)).start()

        early_rows(arrived, q, tail_of(code1_got, q), c1_send.at[q], c1_recv.at[q])
        code2[ways(q * WAYS)] = code1_got[ways(q)]
        each(1, WAYS, codes_on)
        early_rows(arrived, q, rows_of(got1, q), s1_send.at[q], s1_recv.at[q])
        regroup(q)
        got2[q, 0:BLOCK, :] = mid[q, 0:BLOCK, :]
        each(1, WAYS, rows_on)

    def work(q):
        row = iota((LANES, CHUNK_ROWS), 1)
        pick = (iota((LANES, CHUNK_ROWS), 0) == div48(row) * SLOTS + row - 6 * div6(row)).astype(F32).astype(BF16)
        hit = iota((WAYS * WAYS, CHUNK_ROWS), 0) == div6(iota((WAYS * WAYS, CHUNK_ROWS), 1))
        arrived(tiles_of(code2, q), c2_send.at[q], c2_recv.at[q])
        tile = code2[pl.ds(q * PAIRS, PAIRS)].reshape(PAIRS, LANES)
        high, low = codes_from(tile, hit, pick)
        arrived(got2.at[q, pl.ds(BLOCK, CHUNK_ROWS - BLOCK)], s2_send.at[q], s2_recv.at[q])
        members = got2[q]
        spread = spread_of(nearest(members, high), hit, pick)
        for r in range(PAIRS):
            ret1[q * PAIRS + r] = spread[r : r + 1, :]
        ret1_got[ways(q * WAYS)] = ret1[ways(q * WAYS)]

        def back(way):
            at = ways(q * WAYS + way)
            link(ret1.at[at], ret1_got.at[at], r1_send.at[q], r1_recv.at[q], xc_back(way)).start()

        each(1, WAYS, back)
        add_meso(members, high)
        add_fine(members, high, low)

    def pass_back(q):
        def back(way):
            at = q * WAYS + way
            link(ret_mid.at[at], ret2.at[at], r2_send.at[q], r2_recv.at[q], yz_back(q, way)).start()

        arrived(tiles_of(ret1_got, q), r1_send.at[q], r1_recv.at[q])
        ret_mid[ways(q)] = sum(ret1_got[pl.ds((q * WAYS + way) * WAYS, WAYS)] for way in range(WAYS))
        each(start_of(q), WAYS, back)

    def turn(i):
        pass_on(i)

        @pl.when(i > 0)
        def _():
            pass_back(i - 1)

        work(i)

    each(0, SPLIT, turn)

    def early_left(q):
        early_rows(left, q, rows_of(packed, q), s1_send.at[q], s1_recv.at[q])
        early_rows(left, q, tail_of(code1, q), c1_send.at[q], c1_recv.at[q])
        left(mid.at[q, pl.ds(BLOCK, CHUNK_ROWS - BLOCK)], s2_send.at[q], s2_recv.at[q])
        left(tiles_of(code2, q), c2_send.at[q], c2_recv.at[q])
        left(tiles_of(ret1, q), r1_send.at[q], r1_recv.at[q])

    def late_left(q):
        left(packed.at[q, pl.ds(BLOCK, CHUNK_ROWS - BLOCK)], s1_send.at[q], s1_recv.at[q])
        left(tiles_of(last1, q - SPLIT), c1_send.at[q], c1_recv.at[q])

    back_x = [lax.rem(x + NX - dx, NX) for dx in range(NX)]
    back_c = [lax.rem(c + dc, NC) for dc in range(NC)]

    def late_half(n):
        q = SPLIT + lax.div(n, 2)
        h = lax.rem(n, 2)
        late = lax.div(n, 2)
        row = iota((LANES, HALF), 1) + h * HALF
        pick = (iota((LANES, HALF), 0) == row - 48 * div48(row)).astype(F32).astype(BF16)
        hit = iota((WAYS, HALF), 0) == div48(iota((WAYS, HALF), 1) + h * HALF)

        @pl.when(h == 0)
        def _():
            arrived(last2.at[ways(late)], c2_send.at[q], c2_recv.at[q])

        high, low = codes_from(last2[ways(late)].reshape(WAYS, LANES), hit, pick)

        half = pl.ds(pl.multiple_of(h * HALF, HALF), HALF)
        arrived(got2.at[q, half], s2_send.at[q], s2_recv.at[SPLIT + n])
        members = got2[q, half, :]
        add_meso(members, high)

        @pl.when(n == 2 * LATE - 1)
        def _():
            def share_out(dx):
                share = pl.ds(pl.multiple_of(lax.rem(x + dx, NX) * SHARE, SHARE), SHARE)
                device = xc_peer(dx * NC)
                link(part.at[share], part_got.at[dx - 1], p_send, p_recv, device).start()

            each(1, NX, share_out)

        own_hit = iota((WAYS, HALF), 0) == div48(iota((WAYS, HALF), 1))
        spread = spread_of(nearest(members, high), own_hit, pick)
        for r in range(WAYS // 2):
            back1[late * WAYS + h * (WAYS // 2) + r] = spread[r : r + 1, :]

        def back(i):
            way = h * (WAYS // 2) + i
            row = late * WAYS + way
            to_row = EARLY + late * PAIRS + way
            to_yz = (lax.rem(y + NY - q, NY) * NZ + lax.rem(z + NZ - near_z(way), NZ)) * NC
            for j in range(WAYS):
                device = (back_x[j // NC], to_yz + back_c[j % NC])
                link(back1.at[row], ret2.at[to_row + j * WAYS], r2_send.at[q], r2_recv.at[q], device).start()

        each(0, WAYS // 2, back)
        add_fine(members, high, low)

        @pl.when(n == 1)
        def _():
            pass_back(SPLIT - 1)
            each(0, SPLIT, early_left)
            each(SPLIT, CHUNKS, late_left)

    each(0, 2 * LATE, late_half)
    ret2[0] = ret_mid[0]

    inverse[...] = 1.0 / (counts[...] + 1.0)

    arrived(part_got, p_send, p_recv)
    share = pl.ds(pl.multiple_of(x * SHARE, SHARE), SHARE)
    total = (part[share, :] + part_got[1]) + (part_got[0] + part_got[2])
    new_part[...] = (total[:, 0:D] + old[share, :]) / (total[:, D : D + 1] + 1.0)

    def hand_out(dx):
        link(new_part, new_all.at[dx - 1], n_send, n_recv, xc_peer(dx * NC)).start()

    each(1, NX, hand_out)
    new_meso_ref[share, :] = new_part[...]

    def finish(block):
        first_meso = block * SHARE
        for m in range(SHARE):
            rows = pl.ds(pl.multiple_of((first_meso + m) * FGROUP, FGROUP), FGROUP)
            new_fine_ref[rows, :] = (sums[rows, :] + new_meso_ref[pl.ds(first_meso + m, 1), :]) * inverse[rows, :]

    finish(x)

    mine = iota((LANES, ROWS), 0) == jnp.where(is_last, hop1, hop2) * SLOTS + rank
    arrived(ret2.at[pl.ds(1, WAYS - 1)], r2_send.at[0], r2_recv.at[0])
    for q in range(1, SPLIT):
        arrived(ret2.at[ways(q)], r2_send.at[q], r2_recv.at[q])
    for q in range(SPLIT, CHUNKS):
        arrived(ret2.at[pl.ds(EARLY + (q - SPLIT) * PAIRS, PAIRS)], r2_send.at[q], r2_recv.at[q])
    returned = ret2[...].reshape(EARLY + LATE * PAIRS, LANES)
    picked = sum(dot(piece, row_hot[...], TN) for piece in split3(returned))
    near_ref[...] = jnp.sum(jnp.where(mine, picked, 0.0), axis=0, keepdims=True).reshape(ROWS)

    arrived(new_all, n_send, n_recv)

    def finish_other(dx):
        block = lax.rem(x + NX - dx, NX)
        new_meso_ref[pl.ds(pl.multiple_of(block * SHARE, SHARE), SHARE), :] = new_all[dx - 1]
        finish(block)

    each(1, NX, finish_other)

    left(code1.at[pl.ds(1, WAYS - 1)], r2_send.at[0], r2_recv.at[0])
    for q in range(1, SPLIT):
        left(code1.at[ways(q)], r2_send.at[q], r2_recv.at[q])
    for q in range(SPLIT, CHUNKS):
        left(mid.at[q], s2_send.at[q], s2_recv.at[q])
        left(last_mid.at[ways(q - SPLIT)], c2_send.at[q], c2_recv.at[q])
        left(last1.at[pl.ds((q - SPLIT) * PAIRS, PAIRS)], r2_send.at[q], r2_recv.at[q])
    left(part_got, p_send, p_recv)
    left(new_all, n_send, n_recv)


def body(vectors, meso_labels, fine_labels, meso_centroids, fine_centroids):
    hbm = pl.BlockSpec(memory_space=pl.ANY)
    vmem = pl.BlockSpec(memory_space=pltpu.VMEM)
    dma = pltpu.SemaphoreType.DMA
    outs = (((ROWS,), F32), ((MESO_DEV, D), F32), ((MESO_DEV * FGROUP, D), F32))

    def row(count):
        return pltpu.VMEM((count, 1, LANES), F32)

    near, new_meso, new_fine = pl.pallas_call(
        kernel,
        out_shape=tuple(pltpu.VMEM(*out) for out in outs),
        in_specs=[hbm] * 5,
        out_specs=(vmem,) * 3,
        scratch_shapes=[
            pltpu.VMEM((ROWS,), I32),
            pltpu.VMEM((ROWS,), I32),
            pltpu.VMEM((ROWS, D), BF16),
            pltpu.VMEM((MESO_DEV, D), F32),
            pltpu.VMEM((MESO_DEV * KF, D), BF16),
            pltpu.VMEM((MESO_DEV * KF, 1), F32),
            pltpu.VMEM((CHUNK_ROWS, CHUNK_ROWS), BF16),
            pltpu.VMEM((CHUNKS, CHUNK_ROWS, D), BF16),
            pltpu.VMEM((CHUNKS, CHUNK_ROWS, D), BF16),
            pltpu.VMEM((CHUNKS, CHUNK_ROWS, D), BF16),
            pltpu.VMEM((CHUNKS, CHUNK_ROWS, D), BF16),
            row(EARLY), row(EARLY), row(EARLY * WAYS),
            row(LATE * PAIRS), row(LATE * PAIRS), row(LATER), row(LATER),
            row(EARLY * WAYS), row(EARLY * WAYS), row(EARLY),
            row(LATER), row(EARLY + LATE * PAIRS),
            pltpu.VMEM((MESO_DEV * FGROUP, D), F32),
            pltpu.VMEM((MESO_DEV * FGROUP, 1), F32),
            pltpu.VMEM((MESO_DEV, D + LANES), F32),
            pltpu.VMEM((NX - 1, SHARE, D + LANES), F32),
            pltpu.VMEM((SHARE, D), F32),
            pltpu.VMEM((NX - 1, SHARE, D), F32),
            pltpu.VMEM((CHUNK_ROWS, ROWS), BF16),
            pltpu.VMEM((BINS, ROWS), BF16),
            pltpu.VMEM((1, ROWS), I32),
            pltpu.VMEM((1, ROWS), I32),
            pltpu.VMEM((1, ROWS), I32),
            pltpu.VMEM((EARLY + LATE * PAIRS, ROWS), BF16),
            pltpu.VMEM((MESO_DEV * FGROUP, 1), F32),
            dma((5,)),
        ]
        + [dma((CHUNKS,)), dma((CHUNKS,)), dma((CHUNKS,)), dma((SPLIT + 2 * LATE,))]
        + [dma((CHUNKS,)) for _ in range(8)]
        + [dma] * 4
        + [pltpu.SemaphoreType.REGULAR],
        compiler_params=pltpu.CompilerParams(
            collective_id=0, has_side_effects=True, vmem_limit_bytes=61 * 2**20
        ),
    )(
        meso_labels,
        fine_labels,
        vectors,
        meso_centroids,
        fine_centroids.reshape(MESO_DEV * KF, D),
    )
    return (near, new_meso, new_fine.reshape(MESO_DEV, FGROUP, D))


def solution(mesh):
    return jax.shard_map(
        body,
        mesh=mesh,
        in_specs=(
            P(("dp", "owner"), None),
            P(("dp", "owner")),
            P(("dp", "owner")),
            P("owner", None),
            P("owner", None, None),
        ),
        out_specs=(P(("dp", "owner")), P("owner", None), P("owner", "dp", None)),
        check_vma=False,
    )
```

```python
import jax
import jax.numpy as jnp
from jax import lax
from jax.experimental import pallas as pl
from jax.experimental.pallas import tpu as pltpu
from jax.sharding import PartitionSpec as P

MESH = pl.DeviceIdType.MESH
D = 1024
ROWS = 768
KF = 64
MESO_DEV = 32
FGROUP = 16
SLOTS = 6
NX, NY, NZ, NC = 4, 4, 8, 2
CHUNKS = NY
WAYS = 8
BLOCK = WAYS * SLOTS
CHUNK_ROWS = WAYS * BLOCK
BINS = CHUNKS * WAYS * WAYS
LANES = 128
SHARE = MESO_DEV // NX
SPLIT = 2
LATE = CHUNKS - SPLIT
EARLY = SPLIT * WAYS
LATER = LATE * WAYS
PAIRS = WAYS * WAYS
HALF = CHUNK_ROWS // 2

F32, BF16, I32 = jnp.float32, jnp.bfloat16, jnp.int32
NT = (((1,), (1,)), ((), ()))
TN = (((0,), (0,)), ((), ()))


def iota(shape, dim):
    return lax.broadcasted_iota(I32, shape, dim)


def div6(v):
    return (v * 10923) >> 16


def div48(v):
    return div6(v >> 3)


def split3(v):
    first = v.astype(BF16)
    rest = v - first.astype(F32)
    second = rest.astype(BF16)
    third = (rest - second.astype(F32)).astype(BF16)
    return (first, second, third)


def dot(a, b, dims=(((1,), (0,)), ((), ()))):
    return lax.dot_general(a, b, dims, preferred_element_type=F32)


def each(low, high, step):
    def body(i, carry):
        step(i)
        return carry

    lax.fori_loop(low, high, body, 0)


def kernel(
    meso_hbm, fine_hbm, vec_hbm, old_hbm, cent_hbm,
    near_ref, new_meso_ref, new_fine_ref,
    meso_ref, fine_ref, vec, old, cent, half_norm, perm, packed, got1, mid, got2,
    code1, code1_got, code2, last1, last1_got, last_mid, last2,
    ret1, ret1_got, ret_mid, back1, ret2,
    sums, counts, part, part_got, new_part, new_all,
    hot_ref, bin_hot, bin_ref, rank_ref, slot_ref, row_hot, inverse,
    load_sem, s1_send, s1_recv, s2_send, s2_recv, c1_send, c1_recv, c2_send, c2_recv,
    r1_send, r1_recv, r2_send, r2_recv, p_send, p_recv, n_send, n_recv, gate,
):
    x = lax.axis_index("dp")
    own = lax.axis_index("owner")
    y, z, c = lax.div(own, 16), lax.rem(lax.div(own, 2), 8), lax.rem(own, 2)

    def yz_peer(dy, dz):
        return (x, (lax.rem(y + dy, NY) * NZ + lax.rem(z + dz, NZ)) * NC + c)

    def xc_peer(j):
        return (lax.rem(x + lax.div(j, NC), NX), (y * NZ + z) * NC + lax.rem(c + lax.rem(j, NC), NC))

    def xc_back(j):
        return (lax.rem(x + NX - lax.div(j, NC), NX), (y * NZ + z) * NC + lax.rem(c + lax.rem(j, NC), NC))

    def yz_back(dy, dz):
        return yz_peer(NY - dy, NZ - dz)

    def near_z(way):
        odd = lax.rem(way, 2)
        return lax.rem(odd * lax.div(way + 1, 2) + (1 - odd) * lax.div(2 * NZ - way, 2), NZ)

    def start_of(q):
        return lax.div(SPLIT - q, SPLIT)

    def link(src, dst, send_sem, recv_sem, device):
        return pltpu.make_async_remote_copy(
            src_ref=src, dst_ref=dst, send_sem=send_sem, recv_sem=recv_sem,
            device_id=device, device_id_type=MESH,
        )

    here = (x, own)

    def arrived(dst, send_sem, recv_sem):
        link(dst, dst, send_sem, recv_sem, here).wait_recv()

    def left(src, send_sem, recv_sem):
        link(src, src, send_sem, recv_sem, here).wait_send()

    def block(way):
        return pl.ds(pl.multiple_of(way * BLOCK, BLOCK), BLOCK)

    def ways(at):
        return pl.ds(at * WAYS, WAYS)

    barrier = pltpu.get_barrier_semaphore()

    def greet(device):
        pl.semaphore_signal(barrier, 1, device_id=device, device_id_type=MESH)

    for dz in (4, 3, 5, 2, 6, 1, 7):
        greet(yz_peer(0, dz))
    for dy in (2, 1, 3):
        greet(yz_peer(dy, 0))
    for j in range(WAYS - 1, 0, -1):
        greet((lax.rem(x + j // NC, NX), (y * NZ + z) * NC + lax.rem(c + j % NC, NC)))
    greeted = NZ + NY + WAYS - 3

    load_meso = pltpu.make_async_copy(meso_hbm, meso_ref, load_sem.at[3])
    load_fine = pltpu.make_async_copy(fine_hbm, fine_ref, load_sem.at[4])
    load_vec = pltpu.make_async_copy(vec_hbm, vec, load_sem.at[0])
    load_cent = pltpu.make_async_copy(cent_hbm, cent, load_sem.at[1])
    load_old = pltpu.make_async_copy(old_hbm, old, load_sem.at[2])
    for load in (load_meso, load_fine, load_vec, load_cent, load_old):
        load.start()

    load_meso.wait()
    load_fine.wait()
    meso = meso_ref[...].reshape(1, ROWS)
    fine = fine_ref[...].reshape(1, ROWS)
    to = meso >> 5
    dy = ((to >> 4) - y) & 3
    dz = (((to >> 1) & 7) - z) & 7
    way = ((((fine >> 4) - x) & 3) << 1) + ((to - c) & 1)
    z_near = jnp.where(dz <= 4, jnp.maximum(2 * dz - 1, 0), 2 * (NZ - dz))
    is_last = dy >= SPLIT
    hop1 = jnp.where(is_last, way, dz)
    hop2 = jnp.where(is_last, z_near, way)
    first = (dy << 3) + hop1
    bin_of = (first << 3) + hop2
    bin_ref[...] = bin_of

    def bin_rows(i):
        rows = pl.ds(pl.multiple_of(i * 64, 64), 64)
        bin_hot[rows, :] = (iota((64, ROWS), 0) + i * 64 == bin_of).astype(F32).astype(BF16)

    each(0, BINS // 64, bin_rows)

    def ranks(i):
        lanes = pl.ds(pl.multiple_of(i * LANES, LANES), LANES)
        before = (iota((ROWS, LANES), 0) < iota((ROWS, LANES), 1) + i * LANES).astype(F32).astype(BF16)
        ahead = dot(bin_hot[...], before)
        mine = iota((BINS, LANES), 0) == bin_ref[:, lanes]
        rank_ref[:, lanes] = jnp.sum(jnp.where(mine, ahead, 0.0), axis=0, keepdims=True).astype(I32)

    each(0, ROWS // LANES, ranks)
    rank = rank_ref[...]
    slot_ref[...] = bin_of * SLOTS + rank

    meso_code = ((meso & 31) + 1).astype(F32)
    fine_code = (fine & 15).astype(F32)

    def code_rows(hit, lane):
        hot = (iota((LANES, ROWS), 0) == lane).astype(F32).astype(BF16)
        high = jnp.where(hit, meso_code, 0.0).astype(BF16)
        low = jnp.where(hit, fine_code, 0.0).astype(BF16)
        return 16.0 * dot(high, hot, NT) + dot(low, hot, NT)

    codes = code_rows(iota((EARLY, ROWS), 0) == first, hop2 * SLOTS + rank)
    for r in range(EARLY):
        code1[r] = codes[r : r + 1, :]
    load_vec.wait()

    def pack(q):
        def hot_rows(i):
            rows = pl.ds(pl.multiple_of(i * 64, 64), 64)
            at = iota((64, ROWS), 0) + (q * CHUNK_ROWS + i * 64)
            hot_ref[rows, :] = (at == slot_ref[...]).astype(F32).astype(BF16)

        def columns(i):
            lanes = pl.ds(pl.multiple_of(i * 256, 256), 256)
            packed[q, :, lanes] = dot(hot_ref[...], vec[:, lanes]).astype(BF16)

        each(0, CHUNK_ROWS // 64, hot_rows)
        each(0, D // 256, columns)

    def leave_late(q):
        late = q - SPLIT

        def code(way):
            at = ways(late * WAYS + way)
            link(last1.at[at], last1_got.at[at], c1_send.at[q], c1_recv.at[q], xc_peer(way)).start()

        def rows(way):
            link(packed.at[q, block(way)], got1.at[q, block(way)], s1_send.at[q], s1_recv.at[q], xc_peer(way)).start()

        pack(q)
        last1_got[ways(late * WAYS)] = last1[ways(late * WAYS)]
        got1[q, 0:BLOCK, :] = packed[q, 0:BLOCK, :]
        each(1, WAYS, code)
        each(1, WAYS, rows)

    def leave_early(q):
        def code(i):
            way = near_z(i)
            at = q * WAYS + way
            link(code1.at[at], code1_got.at[at], c1_send.at[q], c1_recv.at[q], yz_peer(q, way)).start()

        def rows(i):
            way = near_z(i)
            link(packed.at[q, block(way)], got1.at[q, block(way)], s1_send.at[q], s1_recv.at[q], yz_peer(q, way)).start()

        each(start_of(q), WAYS, code)
        each(start_of(q), WAYS, rows)

    def signal(dy):
        pl.semaphore_signal(gate, 1, device_id=yz_peer(dy, 0), device_id_type=MESH)

    pack(0)
    code1_got[0] = code1[0]
    got1[0, 0:BLOCK, :] = packed[0, 0:BLOCK, :]
    pl.semaphore_wait(barrier, greeted)
    leave_early(0)
    each(1, NY, signal)
    codes = code_rows(iota((LATE * PAIRS, ROWS), 0) + SPLIT * PAIRS == bin_of, hop1 * SLOTS + rank)
    for r in range(LATE * PAIRS):
        last1[r] = codes[r : r + 1, :]
    each(1, SPLIT, pack)
    pl.semaphore_wait(gate, NY - 1)
    each(1, SPLIT, leave_early)
    each(SPLIT, CHUNKS, leave_late)

    def perm_rows(i):
        rows = pl.ds(pl.multiple_of(i * 64, 64), 64)
        out_row = iota((64, CHUNK_ROWS), 0) + i * 64
        in_row = iota((64, CHUNK_ROWS), 1)
        out_pair, in_pair = div6(out_row), div6(in_row)
        swapped = ((out_pair & 7) << 3) + (out_pair >> 3)
        hit = in_row - 6 * in_pair + 6 * swapped == out_row - 6 * out_pair + 6 * in_pair
        perm[rows, :] = hit.astype(F32).astype(BF16)

    each(0, CHUNK_ROWS // 64, perm_rows)

    def regroup(q):
        def columns(i):
            lanes = pl.ds(pl.multiple_of(i * 256, 256), 256)
            mid[q, :, lanes] = dot(perm[...], got1[q, :, lanes]).astype(BF16)

        each(0, D // 256, columns)

    def pass_late(q):
        late = q - SPLIT

        def codes_on(way):
            at = late * WAYS + way
            link(last_mid.at[at], last2.at[at], c2_send.at[q], c2_recv.at[q], yz_peer(q, near_z(way))).start()

        def rows_on(way):
            half = s2_recv.at[SPLIT + late * 2 + lax.div(way, WAYS // 2)]
            link(mid.at[q, block(way)], got2.at[q, block(way)], s2_send.at[q], half, yz_peer(q, near_z(way))).start()

        arrived(last1_got.at[pl.ds(late * PAIRS + WAYS, PAIRS - WAYS)], c1_send.at[q], c1_recv.at[q])
        last_mid[ways(late)] = sum(last1_got[pl.ds(late * PAIRS + way * WAYS, WAYS)] for way in range(WAYS))
        each(0, WAYS, codes_on)
        arrived(got1.at[q, pl.ds(BLOCK, CHUNK_ROWS - BLOCK)], s1_send.at[q], s1_recv.at[q])
        regroup(q)
        each(0, WAYS, rows_on)

    each(SPLIT, CHUNKS, pass_late)

    load_cent.wait()

    def norms(i):
        rows = pl.ds(pl.multiple_of(i * 32, 32), 32)
        wide = cent[rows, :].astype(F32)
        half_norm[rows, :] = 0.5 * jnp.sum(wide * wide, axis=1, keepdims=True)

    each(0, MESO_DEV * KF // 32, norms)

    load_old.wait()

    def begin(m):
        rows = pl.ds(pl.multiple_of(m * FGROUP, FGROUP), FGROUP)
        mine = pl.ds(pl.multiple_of(m * KF + x * FGROUP, FGROUP), FGROUP)
        sums[rows, :] = cent[mine, :].astype(F32) - old[pl.ds(m, 1), :]

    each(0, MESO_DEV, begin)
    from_row = jnp.where(is_last, bin_of - SPLIT * PAIRS + EARLY, first)

    def from_rows(i):
        rows = pl.ds(pl.multiple_of(i * 16, 16), 16)
        row_hot[rows, :] = (iota((16, ROWS), 0) + i * 16 == from_row).astype(F32).astype(BF16)

    each(0, (EARLY + LATE * PAIRS) // 16, from_rows)
    counts[...] = jnp.zeros_like(counts)
    part[...] = jnp.zeros_like(part)

    def codes_from(tile, hit, pick):
        tile = tile.astype(I32)
        high = dot((tile >> 4).astype(F32).astype(BF16), pick)
        low = dot((tile & 15).astype(F32).astype(BF16), pick)
        high = jnp.sum(jnp.where(hit, high, 0.0), axis=0, keepdims=True)
        low = jnp.sum(jnp.where(hit, low, 0.0), axis=0, keepdims=True)
        return (high.astype(I32) - 1, low.astype(I32))

    def add_meso(members, high):
        hot = (iota((MESO_DEV, members.shape[0]), 0) == high).astype(F32)
        part[:, 0:D] += dot(hot.astype(BF16), members)
        part[:, D : D + LANES] += jnp.broadcast_to(jnp.sum(hot, axis=1, keepdims=True), (MESO_DEV, LANES))

    def nearest(members, high):
        size = members.shape[0]
        step = LANES if size % LANES == 0 else size
        eye = iota((step, step), 0) == iota((step, step), 1)
        norm = jnp.concatenate(
            [
                jnp.sum(
                    jnp.where(eye, dot(members[t : t + step], members[t : t + step], NT), 0.0), axis=0, keepdims=True
                )
                for t in range(0, size, step)
            ],
            axis=1,
        )

        best = jnp.zeros((1, size), F32)
        for i in range(0, MESO_DEV * KF, 1024):
            cross = dot(cent[i : i + 1024, :], members, NT) - half_norm[i : i + 1024, :]
            for t in range(0, 1024, KF):
                top = jnp.max(cross[t : t + KF], axis=0, keepdims=True)
                best = jnp.where(high == (i + t) // KF, top, best)
        return jnp.where(high >= 0, (norm - 2.0 * best) * (1.0 / D), 0.0)

    def add_fine(members, high, low):
        code = (high << 4) + low
        size = members.shape[0]

        def step(i):
            rows = pl.ds(pl.multiple_of(i * 128, 128), 128)
            hot = (iota((128, size), 0) + i * 128 == code).astype(F32)
            sums[rows, :] += dot(hot.astype(BF16), members)
            counts[rows, :] += jnp.sum(hot, axis=1, keepdims=True)

        each(0, MESO_DEV * FGROUP // 128, step)

    def spread_of(near, hit, pick):
        return sum(dot(piece, pick, NT) for piece in split3(jnp.where(hit, near, 0.0)))

    def early_rows(step, q, ref, send_sem, recv_sem):
        @pl.when(q == 0)
        def _():
            step(ref(1), send_sem, recv_sem)

        @pl.when(q > 0)
        def _():
            step(ref(0), send_sem, recv_sem)

    def tail_of(ref, q):
        return lambda way: ref.at[pl.ds(q * WAYS + way, WAYS - way)]

    def rows_of(ref, q):
        return lambda way: ref.at[q, pl.ds(way * BLOCK, CHUNK_ROWS - way * BLOCK)]

    def tiles_of(ref, q):
        return ref.at[pl.ds(q * PAIRS + WAYS, PAIRS - WAYS)]

    def pass_on(q):
        def codes_on(way):
            at = q * WAYS + way
            link(code1_got.at[ways(q)], code2.at[ways(at)], c2_send.at[q], c2_recv.at[q], xc_peer(way)).start()

        def rows_on(way):
            link(mid.at[q, block(way)], got2.at[q, block(way)], s2_send.at[q], s2_recv.at[q], xc_peer(way)).start()

        early_rows(arrived, q, tail_of(code1_got, q), c1_send.at[q], c1_recv.at[q])
        code2[ways(q * WAYS)] = code1_got[ways(q)]
        each(1, WAYS, codes_on)
        early_rows(arrived, q, rows_of(got1, q), s1_send.at[q], s1_recv.at[q])
        regroup(q)
        got2[q, 0:BLOCK, :] = mid[q, 0:BLOCK, :]
        each(1, WAYS, rows_on)

    def work(q):
        row = iota((LANES, CHUNK_ROWS), 1)
        pick = (iota((LANES, CHUNK_ROWS), 0) == div48(row) * SLOTS + row - 6 * div6(row)).astype(F32).astype(BF16)
        hit = iota((WAYS * WAYS, CHUNK_ROWS), 0) == div6(iota((WAYS * WAYS, CHUNK_ROWS), 1))
        arrived(tiles_of(code2, q), c2_send.at[q], c2_recv.at[q])
        tile = code2[pl.ds(q * PAIRS, PAIRS)].reshape(PAIRS, LANES)
        high, low = codes_from(tile, hit, pick)
        arrived(got2.at[q, pl.ds(BLOCK, CHUNK_ROWS - BLOCK)], s2_send.at[q], s2_recv.at[q])
        members = got2[q]
        spread = spread_of(nearest(members, high), hit, pick)
        for r in range(PAIRS):
            ret1[q * PAIRS + r] = spread[r : r + 1, :]
        ret1_got[ways(q * WAYS)] = ret1[ways(q * WAYS)]

        def back(way):
            at = ways(q * WAYS + way)
            link(ret1.at[at], ret1_got.at[at], r1_send.at[q], r1_recv.at[q], xc_back(way)).start()

        each(1, WAYS, back)
        add_meso(members, high)
        add_fine(members, high, low)

    def pass_back(q):
        def back(way):
            at = q * WAYS + way
            link(ret_mid.at[at], ret2.at[at], r2_send.at[q], r2_recv.at[q], yz_back(q, way)).start()

        arrived(tiles_of(ret1_got, q), r1_send.at[q], r1_recv.at[q])
        ret_mid[ways(q)] = sum(ret1_got[pl.ds((q * WAYS + way) * WAYS, WAYS)] for way in range(WAYS))
        each(start_of(q), WAYS, back)

    def turn(i):
        pass_on(i)

        @pl.when(i > 0)
        def _():
            pass_back(i - 1)

        work(i)

    each(0, SPLIT, turn)

    def early_left(q):
        early_rows(left, q, rows_of(packed, q), s1_send.at[q], s1_recv.at[q])
        early_rows(left, q, tail_of(code1, q), c1_send.at[q], c1_recv.at[q])
        left(mid.at[q, pl.ds(BLOCK, CHUNK_ROWS - BLOCK)], s2_send.at[q], s2_recv.at[q])
        left(tiles_of(code2, q), c2_send.at[q], c2_recv.at[q])
        left(tiles_of(ret1, q), r1_send.at[q], r1_recv.at[q])

    def late_left(q):
        left(packed.at[q, pl.ds(BLOCK, CHUNK_ROWS - BLOCK)], s1_send.at[q], s1_recv.at[q])
        left(tiles_of(last1, q - SPLIT), c1_send.at[q], c1_recv.at[q])

    back_x = [lax.rem(x + NX - dx, NX) for dx in range(NX)]
    back_c = [lax.rem(c + dc, NC) for dc in range(NC)]

    def late_half(n):
        q = SPLIT + lax.div(n, 2)
        h = lax.rem(n, 2)
        late = lax.div(n, 2)
        row = iota((LANES, HALF), 1) + h * HALF
        pick = (iota((LANES, HALF), 0) == row - 48 * div48(row)).astype(F32).astype(BF16)
        hit = iota((WAYS, HALF), 0) == div48(iota((WAYS, HALF), 1) + h * HALF)

        @pl.when(h == 0)
        def _():
            arrived(last2.at[ways(late)], c2_send.at[q], c2_recv.at[q])

        high, low = codes_from(last2[ways(late)].reshape(WAYS, LANES), hit, pick)

        half = pl.ds(pl.multiple_of(h * HALF, HALF), HALF)
        arrived(got2.at[q, half], s2_send.at[q], s2_recv.at[SPLIT + n])
        members = got2[q, half, :]
        add_meso(members, high)

        @pl.when(n == 2 * LATE - 1)
        def _():
            def share_out(dx):
                share = pl.ds(pl.multiple_of(lax.rem(x + dx, NX) * SHARE, SHARE), SHARE)
                device = xc_peer(dx * NC)
                link(part.at[share], part_got.at[dx - 1], p_send, p_recv, device).start()

            each(1, NX, share_out)

        own_hit = iota((WAYS, HALF), 0) == div48(iota((WAYS, HALF), 1))
        spread = spread_of(nearest(members, high), own_hit, pick)
        for r in range(WAYS // 2):
            back1[late * WAYS + h * (WAYS // 2) + r] = spread[r : r + 1, :]

        def back(i):
            way = h * (WAYS // 2) + i
            row = late * WAYS + way
            to_row = EARLY + late * PAIRS + way
            to_yz = (lax.rem(y + NY - q, NY) * NZ + lax.rem(z + NZ - near_z(way), NZ)) * NC
            for j in range(WAYS):
                device = (back_x[j // NC], to_yz + back_c[j % NC])
                link(back1.at[row], ret2.at[to_row + j * WAYS], r2_send.at[q], r2_recv.at[q], device).start()

        each(0, WAYS // 2, back)
        add_fine(members, high, low)

        @pl.when(n == 1)
        def _():
            pass_back(SPLIT - 1)
            each(0, SPLIT, early_left)
            each(SPLIT, CHUNKS, late_left)

    each(0, 2 * LATE, late_half)
    ret2[0] = ret_mid[0]

    inverse[...] = 1.0 / (counts[...] + 1.0)

    arrived(part_got, p_send, p_recv)
    share = pl.ds(pl.multiple_of(x * SHARE, SHARE), SHARE)
    total = (part[share, :] + part_got[1]) + (part_got[0] + part_got[2])
    new_part[...] = (total[:, 0:D] + old[share, :]) / (total[:, D : D + 1] + 1.0)

    def hand_out(dx):
        link(new_part, new_all.at[dx - 1], n_send, n_recv, xc_peer(dx * NC)).start()

    each(1, NX, hand_out)
    new_meso_ref[share, :] = new_part[...]

    def finish(block):
        first_meso = block * SHARE
        for m in range(SHARE):
            rows = pl.ds(pl.multiple_of((first_meso + m) * FGROUP, FGROUP), FGROUP)
            new_fine_ref[rows, :] = (sums[rows, :] + new_meso_ref[pl.ds(first_meso + m, 1), :]) * inverse[rows, :]

    finish(x)

    mine = iota((LANES, ROWS), 0) == jnp.where(is_last, hop1, hop2) * SLOTS + rank
    arrived(ret2.at[pl.ds(1, WAYS - 1)], r2_send.at[0], r2_recv.at[0])
    for q in range(1, SPLIT):
        arrived(ret2.at[ways(q)], r2_send.at[q], r2_recv.at[q])
    for q in range(SPLIT, CHUNKS):
        arrived(ret2.at[pl.ds(EARLY + (q - SPLIT) * PAIRS, PAIRS)], r2_send.at[q], r2_recv.at[q])
    returned = ret2[...].reshape(EARLY + LATE * PAIRS, LANES)
    picked = sum(dot(piece, row_hot[...], TN) for piece in split3(returned))
    near_ref[...] = jnp.sum(jnp.where(mine, picked, 0.0), axis=0, keepdims=True).reshape(ROWS)

    arrived(new_all, n_send, n_recv)

    def finish_other(dx):
        block = lax.rem(x + NX - dx, NX)
        new_meso_ref[pl.ds(pl.multiple_of(block * SHARE, SHARE), SHARE), :] = new_all[dx - 1]
        finish(block)

    each(1, NX, finish_other)

    left(code1.at[pl.ds(1, WAYS - 1)], r2_send.at[0], r2_recv.at[0])
    for q in range(1, SPLIT):
        left(code1.at[ways(q)], r2_send.at[q], r2_recv.at[q])
    for q in range(SPLIT, CHUNKS):
        left(mid.at[q], s2_send.at[q], s2_recv.at[q])
        left(last_mid.at[ways(q - SPLIT)], c2_send.at[q], c2_recv.at[q])
        left(last1.at[pl.ds((q - SPLIT) * PAIRS, PAIRS)], r2_send.at[q], r2_recv.at[q])
    left(part_got, p_send, p_recv)
    left(new_all, n_send, n_recv)


def body(vectors, meso_labels, fine_labels, meso_centroids, fine_centroids):
    hbm = pl.BlockSpec(memory_space=pl.ANY)
    vmem = pl.BlockSpec(memory_space=pltpu.VMEM)
    dma = pltpu.SemaphoreType.DMA
    outs = (((ROWS,), F32), ((MESO_DEV, D), F32), ((MESO_DEV * FGROUP, D), F32))

    def row(count):
        return pltpu.VMEM((count, 1, LANES), F32)

    near, new_meso, new_fine = pl.pallas_call(
        kernel,
        out_shape=tuple(pltpu.VMEM(*out) for out in outs),
        in_specs=[hbm] * 5,
        out_specs=(vmem,) * 3,
        scratch_shapes=[
            pltpu.VMEM((ROWS,), I32),
            pltpu.VMEM((ROWS,), I32),
            pltpu.VMEM((ROWS, D), BF16),
            pltpu.VMEM((MESO_DEV, D), F32),
            pltpu.VMEM((MESO_DEV * KF, D), BF16),
            pltpu.VMEM((MESO_DEV * KF, 1), F32),
            pltpu.VMEM((CHUNK_ROWS, CHUNK_ROWS), BF16),
            pltpu.VMEM((CHUNKS, CHUNK_ROWS, D), BF16),
            pltpu.VMEM((CHUNKS, CHUNK_ROWS, D), BF16),
            pltpu.VMEM((CHUNKS, CHUNK_ROWS, D), BF16),
            pltpu.VMEM((CHUNKS, CHUNK_ROWS, D), BF16),
            row(EARLY), row(EARLY), row(EARLY * WAYS),
            row(LATE * PAIRS), row(LATE * PAIRS), row(LATER), row(LATER),
            row(EARLY * WAYS), row(EARLY * WAYS), row(EARLY),
            row(LATER), row(EARLY + LATE * PAIRS),
            pltpu.VMEM((MESO_DEV * FGROUP, D), F32),
            pltpu.VMEM((MESO_DEV * FGROUP, 1), F32),
            pltpu.VMEM((MESO_DEV, D + LANES), F32),
            pltpu.VMEM((NX - 1, SHARE, D + LANES), F32),
            pltpu.VMEM((SHARE, D), F32),
            pltpu.VMEM((NX - 1, SHARE, D), F32),
            pltpu.VMEM((CHUNK_ROWS, ROWS), BF16),
            pltpu.VMEM((BINS, ROWS), BF16),
            pltpu.VMEM((1, ROWS), I32),
            pltpu.VMEM((1, ROWS), I32),
            pltpu.VMEM((1, ROWS), I32),
            pltpu.VMEM((EARLY + LATE * PAIRS, ROWS), BF16),
            pltpu.VMEM((MESO_DEV * FGROUP, 1), F32),
            dma((5,)),
        ]
        + [dma((CHUNKS,)), dma((CHUNKS,)), dma((CHUNKS,)), dma((SPLIT + 2 * LATE,))]
        + [dma((CHUNKS,)) for _ in range(8)]
        + [dma] * 4
        + [pltpu.SemaphoreType.REGULAR],
        compiler_params=pltpu.CompilerParams(
            collective_id=0, has_side_effects=True, vmem_limit_bytes=61 * 2**20
        ),
    )(
        meso_labels,
        fine_labels,
        vectors,
        meso_centroids,
        fine_centroids.reshape(MESO_DEV * KF, D),
    )
    return (near, new_meso, new_fine.reshape(MESO_DEV, FGROUP, D))


def solution(mesh):
    return jax.shard_map(
        body,
        mesh=mesh,
        in_specs=(
            P(("dp", "owner"), None),
            P(("dp", "owner")),
            P(("dp", "owner")),
            P("owner", None),
            P("owner", None, None),
        ),
        out_specs=(P(("dp", "owner")), P("owner", None), P("owner", "dp", None)),
        check_vma=False,
    )
```
